512 devices in a mesh: gx: 16 (over z), gy: 8 (over x, core), sa: 4 (over y).
Axes of the slice: x: 4, y: 4, z: 16, core: 2. Of those that a mesh axis runs over, the one named last changes fastest.
Arguments:
- profile_fields: float32 [32, 4, 524288], P(None, None, ('gx', 'gy', 'sa')), may hold values from -6 to 6
- turbulent_coefficients: float32 [32, 2, 524288], P(None, None, ('gx', 'gy', 'sa')), may hold values from 0.3 to 6
- column_patch_owner: int32 [2, 524288], P(None, ('gx', 'gy', 'sa')), may hold values from 0 to 1023, as said below
- kind_fractions: float32 [6, 524288], P(None, ('gx', 'gy', 'sa')), may hold values from 0.1 to 1
- kind_existing_flags: int32 [5, 524288], P(None, ('gx', 'gy', 'sa')), may hold values 0 or 1
- kind_absorbed_flux: float32 [6, 524288], P(None, ('gx', 'gy', 'sa')), may hold values from -6 to 6
- kind_thermal_links: float32 [6, 524288], P(None, ('gx', 'gy', 'sa')), may hold values from 0.2 to 3
- bottom_kelvin: float32 [6, 524288], P(None, ('gx', 'gy', 'sa')), may hold values from -5 to 5
- drift_speeds: float32 [2, 524288], P(None, ('gx', 'gy', 'sa')), may hold values from -5 to 5
Outputs:
- advanced_profile: float32 [32, 4, 524288], P(None, None, ('gx', 'gy', 'sa'))
- kind_interface_kelvin: float32 [6, 524288], P(None, ('gx', 'gy', 'sa'))
The draws below stay inside these ranges and needn't reach their ends.
Inputs may be any that keep to these rules, and one draw needn't show every extreme that they name: column_patch_owner[0, i] * 1024 + column_patch_owner[1, i] over all columns i is a permutation of the 524288 cells; row 0 is below 512 and row 1 below 1024. Cell j is held by the device that holds entry j of the cell arrays. The columns of one device have their cells on every device, 1 to 4 of them on each, and exactly 4 on some device.
All inputs are finite; a program needn't handle non-finite values. No bound on the sum of `kind_existing_flags` on one device may be relied on, other than what follows from the above.
Results may differ from the reference program's by a relative error of at most 0.00016.
Values sent between devices are 32-bit elements; how exact they have to be, the bound alone decides.
No kernel may reach another device: no remote copies, remote signals or barrier semaphores. Data moves between devices by JAX's collectives and lax.ppermute only.
A program may use at most 64 MiB of HBM per device.

```python
import math
import jax
import jax.numpy as jnp
from jax import lax

COL_DEV = 1024
LEV = 32
SWEEPS = 3
COLS = 524288
GROUND_PATCHES = 524288
CAP = 4


def draw_column_patch_owner(key, part):
    device_total = COLS // COL_DEV
    unit_total = device_total * (CAP - 1)
    base_key = jax.random.fold_in(key, 17)
    subkeys = jax.random.split(base_key, 6)
    full_group = jax.random.randint(subkeys[0], (), 0, device_total)
    unit_ids = jnp.arange(unit_total, dtype=jnp.int32)
    scores = jax.random.randint(subkeys[1], (unit_total,), 0, unit_total) * unit_total + unit_ids
    scores = jnp.where(unit_ids // (CAP - 1) == full_group, unit_ids - unit_total * unit_total, scores)
    ranked = jnp.argsort(scores)
    chosen = jnp.zeros((unit_total,), jnp.int32).at[ranked[:COL_DEV - device_total]].set(1)
    group_sizes = 1 + jnp.sum(chosen.reshape(device_total, CAP - 1), axis=1)
    group_ends = jnp.cumsum(group_sizes)
    position = jnp.arange(COL_DEV, dtype=jnp.int32)
    group_of = jnp.sum((position[:, None] >= group_ends[None, :]).astype(jnp.int32), axis=1)
    source_rank = jax.random.permutation(subkeys[2], device_total)
    owner_perm = jax.random.permutation(subkeys[3], device_total)
    owner_dev = owner_perm[(source_rank[:, None] + group_of[None, :]) % device_total]
    slot_perm = jax.vmap(lambda subkey: jax.random.permutation(subkey, COL_DEV))(jax.random.split(subkeys[4], device_total))
    cell_local = slot_perm.reshape(-1)[owner_dev * COL_DEV + position[None, :]]
    column_perm = jax.vmap(lambda subkey: jax.random.permutation(subkey, COL_DEV))(jax.random.split(subkeys[5], device_total))
    owner_out = jnp.take_along_axis(owner_dev, column_perm, axis=1).reshape(-1)
    local_out = jnp.take_along_axis(cell_local, column_perm, axis=1).reshape(-1)
    return jnp.stack([owner_out, local_out], axis=0).astype(jnp.int32)


def place_ends(array, stream_key, least, top_value):
    index_at = [jax.random.randint(jax.random.fold_in(stream_key, axis), (), 0, length) for axis, length in enumerate(array.shape)]
    main_axis = array.shape.index(max(array.shape))
    neighbour = index_at[:main_axis] + [(index_at[main_axis] + 1) % array.shape[main_axis]] + index_at[main_axis + 1:]
    return array.at[tuple(index_at)].set(least).at[tuple(neighbour)].set(top_value)


def steps_of(rng, dims, cuts, low, high):
    loudness = 1.0
    for dim, blocks in cuts:
        draws = jax.random.uniform(jax.random.fold_in(jax.random.fold_in(rng, 6), dim), (blocks,), jnp.float32, low / len(cuts), high / len(cuts))
        loudness = loudness * jnp.repeat(jnp.exp(draws), dims[dim] // blocks).reshape((-1,) + (1,) * (len(dims) - 1 - dim))
    return loudness


def normal_values(own_key, shape, spread, bound, shards=(), kind=jnp.bfloat16):
    result = spread * jax.random.normal(own_key, shape, jnp.float32)
    if shards:
        result = result * steps_of(own_key, shape, shards, -0.22, 0.18)
    return jnp.clip(result, -bound, bound).astype(kind)


def setup_inputs(seed: int = 0) -> dict:
    key_of = jax.random.split(jax.random.key(seed), 10)
    profile_fields = normal_values(key_of[0], (LEV, 4, COLS), 1.0, 6.0, ((2, 512),), jnp.float32)
    turbulent_coefficients = jnp.clip(jnp.exp(math.log(6.0) - 2.9957322 * jax.random.uniform(key_of[1], (LEV, 2, COLS), jnp.float32) ** steps_of(key_of[1], (LEV, 2, COLS), ((2, 512),), -0.2, 0.2)), 0.3, 6.0)
    column_patch_owner = draw_column_patch_owner(jax.random.fold_in(key_of[9], 71), 0)
    kind_fractions = jnp.clip(jnp.exp(math.log(1.0) - 2.3025851 * jax.random.uniform(key_of[3], (6, GROUND_PATCHES), jnp.float32) ** steps_of(key_of[3], (6, GROUND_PATCHES), ((1, 512),), -0.2, 0.2)), 0.1, 1.0)
    kind_existing_flags = place_ends((jax.random.randint(key_of[4], (5, GROUND_PATCHES), 0, 2) < 1).astype(jnp.int32), jax.random.fold_in(key_of[4], 1), 0, 1)
    kind_absorbed_flux = normal_values(key_of[5], (6, GROUND_PATCHES), 1.5, 6.0, ((1, 512),), jnp.float32)
    kind_thermal_links = jnp.clip(jnp.exp(math.log(3.0) - 2.7080502 * jax.random.uniform(key_of[6], (6, GROUND_PATCHES), jnp.float32) ** steps_of(key_of[6], (6, GROUND_PATCHES), ((1, 512),), -0.2, 0.2)), 0.2, 3.0)
    bottom_kelvin = normal_values(key_of[7], (6, GROUND_PATCHES), 1.0, 5.0, ((1, 512),), jnp.float32)
    drift_speeds = normal_values(key_of[8], (2, GROUND_PATCHES), 1.0, 5.0, ((1, 512),), jnp.float32)
    return dict(profile_fields=profile_fields, turbulent_coefficients=turbulent_coefficients, column_patch_owner=column_patch_owner, kind_fractions=kind_fractions, kind_existing_flags=kind_existing_flags, kind_absorbed_flux=kind_absorbed_flux, kind_thermal_links=kind_thermal_links, bottom_kelvin=bottom_kelvin, drift_speeds=drift_speeds)


VAPOUR_ENTHALPY = 2.5


def vapour_limit(values):
    return 0.6 * jnp.exp(0.3 * values)


def longwave_outgoing(values):
    return 0.5 * jnp.exp(0.2 * values)


def eliminate(values, coupling):
    def advance(carried, inputs):
        offset_prev, factor_prev, above_coef = carried
        level_values, below_coef = inputs
        divisor = 1.0 + above_coef * (1.0 - factor_prev) + below_coef
        offset_now = (level_values + above_coef * offset_prev) / divisor
        factor_now = below_coef / divisor
        return (offset_now, factor_now, below_coef), (offset_now, factor_now)

    zeros_row = jnp.zeros_like(values[0])
    _, (sweep_shifts, sweep_multipliers) = lax.scan(advance, (zeros_row, zeros_row, zeros_row), (values, coupling))
    return sweep_shifts, sweep_multipliers


def substitute(sweep_shifts, sweep_multipliers, boundary):
    def advance(level_below, inputs):
        level_offset, level_factor = inputs
        solved = level_offset + level_factor * level_below
        return solved, solved

    _, solved = lax.scan(advance, boundary, (sweep_shifts, sweep_multipliers), reverse=True)
    return solved


def surface_weights(kind_fractions, kind_existing_flags):
    present = jnp.concatenate([jnp.ones_like(kind_existing_flags[:1]), kind_existing_flags], axis=0).astype(kind_fractions.dtype)
    unscaled = kind_fractions * present
    return unscaled / jnp.sum(unscaled, axis=0, keepdims=True)


def flux_budget(cell_fields, heat_offset, heat_factor, moist_offset, moist_factor, transfer_factor):
    fraction_shares = cell_fields[0:6]
    absorbed_flux = cell_fields[6:12]
    thermal_link = cell_fields[12:18]
    bottom_layer = cell_fields[18:24]
    interface_kelvin = bottom_layer
    for sweep_index in range(SWEEPS):
        humidity_limit = vapour_limit(interface_kelvin)
        averaged_enthalpy = jnp.sum(fraction_shares * interface_kelvin, axis=0)
        averaged_humidity = jnp.sum(fraction_shares * humidity_limit, axis=0)
        lowest_enthalpy = heat_offset + heat_factor * averaged_enthalpy
        lowest_humidity = moist_offset + moist_factor * averaged_humidity
        outgoing_flux = longwave_outgoing(interface_kelvin)
        budget_residual = (absorbed_flux - outgoing_flux - transfer_factor * (interface_kelvin - lowest_enthalpy)
                     - VAPOUR_ENTHALPY * transfer_factor * (humidity_limit - lowest_humidity) - thermal_link * (interface_kelvin - bottom_layer))
        budget_slope = 0.2 * outgoing_flux + transfer_factor * (1.0 + VAPOUR_ENTHALPY * 0.3 * humidity_limit) + thermal_link
        interface_kelvin = interface_kelvin + budget_residual / budget_slope
    humidity_limit = vapour_limit(interface_kelvin)
    return interface_kelvin, jnp.sum(fraction_shares * interface_kelvin, axis=0), jnp.sum(fraction_shares * humidity_limit, axis=0)


def reference(profile_fields, turbulent_coefficients, column_patch_owner, kind_fractions, kind_existing_flags, kind_absorbed_flux, kind_thermal_links, bottom_kelvin, drift_speeds):
    coupling = jnp.repeat(turbulent_coefficients, 2, axis=1)
    sweep_shifts, sweep_multipliers = eliminate(profile_fields, coupling)
    fraction_shares = surface_weights(kind_fractions, kind_existing_flags)
    patch_locator = (column_patch_owner[0] * COL_DEV + column_patch_owner[1]).astype(jnp.int32)
    patch_directory = jnp.concatenate([fraction_shares, kind_absorbed_flux, kind_thermal_links, bottom_kelvin, drift_speeds], axis=0)
    gathered_fields = patch_directory[:, patch_locator]
    interface_kelvin, averaged_enthalpy, averaged_humidity = flux_budget(gathered_fields, sweep_shifts[-1, 0], sweep_multipliers[-1, 0], sweep_shifts[-1, 1], sweep_multipliers[-1, 1], turbulent_coefficients[-1, 0])
    kind_interface_kelvin = jnp.zeros_like(bottom_kelvin).at[:, patch_locator].set(interface_kelvin)
    boundary = jnp.stack([averaged_enthalpy, averaged_humidity, gathered_fields[24], gathered_fields[25]], axis=0)
    advanced_profile = substitute(sweep_shifts, sweep_multipliers, boundary)
    return advanced_profile, kind_interface_kelvin
```

```python
import jax
import jax.numpy as jnp
from jax import lax
from jax.experimental import pallas as pl
from jax.experimental.pallas import tpu as pltpu
from jax.sharding import PartitionSpec as P

SWEEPS = 3
WORDS = 8
CAP = 4
LANES = 128
VAPOUR_ENTHALPY = 2.5
NT = (((1,), (1,)), ((), ()))
NN = (((1,), (0,)), ((), ()))


def halves(x):
    high = x.astype(jnp.bfloat16)
    return high, (x - high.astype(jnp.float32)).astype(jnp.bfloat16)


def one_hot(index_row, count):
    ids = lax.broadcasted_iota(jnp.int32, (count, index_row.shape[1]), 0)
    return jnp.where(ids == index_row, 1.0, 0.0).astype(jnp.bfloat16)


def dot(a, b, dims):
    return lax.dot_general(a, b, dims, preferred_element_type=jnp.float32)


def columns_kernel(far, near, prof_ref, coef_ref, owner_ref, off_ref, fac_ref, send_ref, slot_ref):
    levels, fields, n = prof_ref.shape
    scalar_row = lax.broadcasted_iota(jnp.int32, (fields, n), 0) < 2
    owner = owner_ref[0:1, :]
    blocks = n // LANES
    tall = jnp.concatenate([owner[:, j * LANES:(j + 1) * LANES] for j in range(blocks)], axis=0).T
    earlier = lax.broadcasted_iota(jnp.int32, (LANES, LANES), 0) < lax.broadcasted_iota(jnp.int32, (LANES, LANES), 1)
    totals = [jnp.zeros((1, LANES), jnp.int32) for _ in range(blocks)]
    for i in range(blocks):
        source = jnp.broadcast_to(tall[:, i:i + 1], (LANES, LANES))
        for j in range(i, blocks):
            same = source == owner[:, j * LANES:(j + 1) * LANES]
            if i == j:
                same = same & earlier
            totals[j] += jnp.sum(same.astype(jnp.int32), axis=0, keepdims=True)
    slot = owner * CAP + jnp.concatenate(totals, axis=1)
    slot_ref[...] = slot

    above = factor = offset = jnp.zeros((fields, n), jnp.float32)
    for k in range(levels):
        below = jnp.where(scalar_row, coef_ref[k, 0:1, :], coef_ref[k, 1:2, :])
        inverse = 1.0 / (1.0 + above * (1.0 - factor) + below)
        offset = (prof_ref[k] + above * offset) * inverse
        factor = below * inverse
        above = below
        off_ref[k] = offset
        fac_ref[k] = factor

    values = jnp.concatenate(
        [
            (owner_ref[1:2, :] + 1).astype(jnp.float32),
            offset[0:2],
            factor[0:1],
            above[0:1],
            jnp.zeros((WORDS - 5, n), jnp.float32),
        ],
        axis=0,
    )
    per_far = near * CAP
    row = slot // per_far
    spread = jnp.concatenate([jnp.where(row == g, values, 0.0) for g in range(far)], axis=0)
    place = one_hot(slot % per_far, per_far)
    sent = dot(jnp.concatenate(halves(spread), axis=0), place, NT)
    rows = far * WORDS
    send_ref[...] = (sent[:rows] + sent[rows:]).reshape(far, WORDS, per_far)


def cells_kernel(got_ref, share_ref, flux_ref, link_ref, bottom_ref, drift_ref, kelvin_ref, reply_ref):
    far = reply_ref.shape[0]
    per_far = reply_ref.shape[2]
    n = share_ref.shape[1]
    blocks = n // LANES
    got = got_ref[...].reshape(per_far, far * WORDS).T
    got = jnp.concatenate([got[g * WORDS:(g + 1) * WORDS] for g in range(far)], axis=1)
    cell = got[0:1].astype(jnp.int32) - 1
    block = cell // LANES
    block = jnp.where(cell < 0, -1, block)
    place = one_hot(cell % LANES, LANES)
    spread = jnp.concatenate([jnp.where(block == b, got, 0.0) for b in range(blocks)], axis=0)
    rows = blocks * WORDS
    held = dot(jnp.concatenate(halves(spread), axis=0), place, NT)
    held = held[:rows] + held[rows:]
    held = jnp.concatenate([held[b * WORDS:(b + 1) * WORDS] for b in range(blocks)], axis=1)
    heat_offset, moist_offset, factor, exchange = (held[k:k + 1] for k in range(1, 5))

    share, flux, link, bottom = share_ref[...], flux_ref[...], link_ref[...], bottom_ref[...]
    temp = bottom
    for _ in range(SWEEPS):
        sat = 0.6 * jnp.exp(0.3 * temp)
        air_heat = heat_offset + factor * jnp.sum(share * temp, axis=0, keepdims=True)
        air_moist = moist_offset + factor * jnp.sum(share * sat, axis=0, keepdims=True)
        emitted = 0.5 * jnp.exp(0.2 * temp)
        residual = (
            flux
            - emitted
            - exchange * (temp - air_heat)
            - VAPOUR_ENTHALPY * exchange * (sat - air_moist)
            - link * (temp - bottom)
        )
        slope = 0.2 * emitted + exchange * (1.0 + VAPOUR_ENTHALPY * 0.3 * sat) + link
        temp = temp + residual / slope
    kelvin_ref[...] = temp
    answer = jnp.concatenate(
        [
            jnp.sum(share * temp, axis=0, keepdims=True),
            jnp.sum(share * (0.6 * jnp.exp(0.3 * temp)), axis=0, keepdims=True),
            drift_ref[...],
            jnp.zeros((WORDS - 4, n), jnp.float32),
        ],
        axis=0,
    )
    answer = jnp.concatenate([answer[:, b * LANES:(b + 1) * LANES] for b in range(blocks)], axis=0)
    spread = dot(jnp.concatenate(halves(answer), axis=1), jnp.concatenate([place, place], axis=0), NN)
    reply = jnp.zeros((WORDS, far * per_far), jnp.float32)
    for b in range(blocks):
        reply = reply + jnp.where(block == b, spread[b * WORDS:(b + 1) * WORDS], 0.0)
    for g in range(far):
        reply_ref[g] = reply[:, g * per_far:(g + 1) * per_far]


def finish_kernel(back_ref, slot_ref, off_ref, fac_ref, out_ref):
    levels, fields, n = off_ref.shape
    near, cap, width = back_ref.shape
    per_far = near * cap
    far = width // WORDS
    slot = slot_ref[...]
    row = slot // per_far
    place = one_hot(slot % per_far, per_far)
    back = back_ref[...].reshape(per_far, width).T
    spread = dot(jnp.concatenate(halves(back), axis=1), jnp.concatenate([place, place], axis=0), NN)
    level = jnp.zeros((WORDS, n), jnp.float32)
    for g in range(far):
        level = level + jnp.where(row == g, spread[g * WORDS:(g + 1) * WORDS], 0.0)
    level = level[0:fields]
    for k in range(levels - 1, -1, -1):
        level = off_ref[k] + fac_ref[k] * level
        out_ref[k] = level


def call(kernel, out_shape, *args):
    vmem = pl.BlockSpec(memory_space=pltpu.VMEM)
    return pl.pallas_call(
        kernel,
        out_shape=out_shape,
        in_specs=[vmem] * len(args),
        out_specs=jax.tree.map(lambda _: vmem, out_shape),
        compiler_params=pltpu.CompilerParams(vmem_limit_bytes=40 * 1024 * 1024),
    )(*args)


def surface_weights(kind_fractions, kind_existing_flags):
    present = jnp.concatenate(
        [jnp.ones_like(kind_existing_flags[:1]), kind_existing_flags], axis=0
    ).astype(jnp.float32)
    unscaled = kind_fractions * present
    return unscaled / jnp.sum(unscaled, axis=0, keepdims=True)


def exchange_parcels(parcels, near):
    far = parcels.shape[0]
    parcels = lax.all_to_all(parcels, "gx", split_axis=0, concat_axis=0, tiled=True)
    parcels = parcels.reshape(far * WORDS, near * CAP).T.reshape(near, CAP, far * WORDS)
    return lax.all_to_all(parcels, ("gy", "sa"), split_axis=0, concat_axis=0, tiled=True)


def per_device(profile, coefficients, owner, fractions, flags, flux, links, bottom, drift):
    far = lax.axis_size("gx")
    near = lax.axis_size(("gy", "sa"))
    n = profile.shape[2]
    f32 = jnp.float32
    shape = jax.ShapeDtypeStruct
    share = surface_weights(fractions, flags)
    parcels = shape((far, WORDS, near * CAP), f32)
    offsets, factors, send, slot = call(
        lambda *refs: columns_kernel(far, near, *refs),
        (shape(profile.shape, f32), shape(profile.shape, f32), parcels, shape((1, n), jnp.int32)),
        profile, coefficients, owner,
    )
    got = exchange_parcels(send, near)
    kelvin, reply = call(
        cells_kernel, (shape(bottom.shape, f32), parcels), got, share, flux, links, bottom, drift
    )
    back = exchange_parcels(reply, near)
    advanced = call(finish_kernel, shape(profile.shape, f32), back, slot, offsets, factors)
    return advanced, kelvin


def solution(mesh):
    spread3 = P(None, None, ("gx", "gy", "sa"))
    spread2 = P(None, ("gx", "gy", "sa"))
    return jax.shard_map(
        per_device,
        mesh=mesh,
        in_specs=(spread3, spread3) + (spread2,) * 7,
        out_specs=(spread3, spread2),
        check_vma=False,
    )
```

```python
import jax
import jax.numpy as jnp
from jax import lax
from jax.experimental import pallas as pl
from jax.experimental.pallas import tpu as pltpu
from jax.sharding import PartitionSpec as P

SWEEPS = 3
WORDS = 8
CAP = 4
LANES = 128
PIECES = 4
VAPOUR_ENTHALPY = 2.5
NT = (((1,), (1,)), ((), ()))
NN = (((1,), (0,)), ((), ()))


def halves(x):
    high = x.astype(jnp.bfloat16)
    return high, (x - high.astype(jnp.float32)).astype(jnp.bfloat16)


def one_hot(index_row, count):
    ids = lax.broadcasted_iota(jnp.int32, (count, index_row.shape[1]), 0)
    return jnp.where(ids == index_row, 1.0, 0.0).astype(jnp.bfloat16)


def dot(a, b, dims):
    return lax.dot_general(a, b, dims, preferred_element_type=jnp.float32)


def columns_kernel(
    far,
    near,
    prof_hbm,
    coef_hbm,
    owner_hbm,
    fraction_hbm,
    flag_hbm,
    flux_hbm,
    link_hbm,
    bottom_hbm,
    drift_hbm,
    off_ref,
    fac_ref,
    send_ref,
    slot_ref,
    share_ref,
    flux_ref,
    link_ref,
    bottom_ref,
    drift_ref,
    prof_ref,
    coef_ref,
    owner_ref,
    fraction_ref,
    flag_ref,
    sems,
):
    pairs = (
        (owner_hbm, owner_ref),
        (coef_hbm, coef_ref),
        (prof_hbm, prof_ref),
        (fraction_hbm, fraction_ref),
        (flag_hbm, flag_ref),
        (flux_hbm, flux_ref),
        (link_hbm, link_ref),
        (bottom_hbm, bottom_ref),
        (drift_hbm, drift_ref),
    )
    copies = [pltpu.make_async_copy(a, b, sems.at[k]) for k, (a, b) in enumerate(pairs)]
    for copy in copies:
        copy.start()
    levels, fields, n = prof_ref.shape
    scalar_row = lax.broadcasted_iota(jnp.int32, (fields, n), 0) < 2
    copies[0].wait()
    owner = owner_ref[0:1, :]
    blocks = n // LANES
    tall = jnp.concatenate([owner[:, j * LANES:(j + 1) * LANES] for j in range(blocks)], axis=0).T
    earlier = lax.broadcasted_iota(jnp.int32, (LANES, LANES), 0) < lax.broadcasted_iota(jnp.int32, (LANES, LANES), 1)
    totals = [jnp.zeros((1, LANES), jnp.int32) for _ in range(blocks)]
    for i in range(blocks):
        source = jnp.broadcast_to(tall[:, i:i + 1], (LANES, LANES))
        for j in range(i, blocks):
            same = source == owner[:, j * LANES:(j + 1) * LANES]
            if i == j:
                same = same & earlier
            totals[j] += jnp.sum(same.astype(jnp.int32), axis=0, keepdims=True)
    slot = owner * CAP + jnp.concatenate(totals, axis=1)
    slot_ref[...] = slot
    per_far = near * CAP
    row = slot // per_far
    place = one_hot(slot % per_far, per_far)

    copies[1].wait()
    copies[2].wait()
    above = factor = offset = jnp.zeros((fields, n), jnp.float32)
    for k in range(levels):
        below = jnp.where(scalar_row, coef_ref[k, 0:1, :], coef_ref[k, 1:2, :])
        inverse = 1.0 / (1.0 + above * (1.0 - factor) + below)
        offset = (prof_ref[k] + above * offset) * inverse
        factor = below * inverse
        above = below
        off_ref[k] = offset
        fac_ref[k] = factor

    values = jnp.concatenate(
        [
            (owner_ref[1:2, :] + 1).astype(jnp.float32),
            offset[0:2],
            factor[0:1],
            above[0:1],
            jnp.zeros((WORDS - 5, n), jnp.float32),
        ],
        axis=0,
    )
    spread = jnp.concatenate([jnp.where(row == g, values, 0.0) for g in range(far)], axis=0)
    sent = dot(jnp.concatenate(halves(spread), axis=0), place, NT)
    rows = far * WORDS
    send_ref[...] = (sent[:rows] + sent[rows:]).reshape(far, WORDS, per_far)

    copies[3].wait()
    copies[4].wait()
    water = fraction_ref[0:1, :]
    ice = fraction_ref[1:, :] * flag_ref[...].astype(jnp.float32)
    inverse = 1.0 / (water + jnp.sum(ice, axis=0, keepdims=True))
    share_ref[0:1, :] = water * inverse
    share_ref[1:, :] = ice * inverse
    for copy in copies[5:]:
        copy.wait()


def cells_kernel(got_ref, share_ref, flux_ref, link_ref, bottom_ref, drift_ref, kelvin_ref, reply_ref):
    far = reply_ref.shape[0]
    per_far = reply_ref.shape[2]
    n = share_ref.shape[1]
    blocks = n // LANES
    got = got_ref[...].reshape(per_far, far * WORDS).T
    got = jnp.concatenate([got[g * WORDS:(g + 1) * WORDS] for g in range(far)], axis=1)
    cell = got[0:1].astype(jnp.int32) - 1
    block = cell // LANES
    block = jnp.where(cell < 0, -1, block)
    place = one_hot(cell % LANES, LANES)
    spread = jnp.concatenate([jnp.where(block == b, got, 0.0) for b in range(blocks)], axis=0)
    rows = blocks * WORDS
    held = dot(jnp.concatenate(halves(spread), axis=0), place, NT)
    held = held[:rows] + held[rows:]
    held = jnp.concatenate([held[b * WORDS:(b + 1) * WORDS] for b in range(blocks)], axis=1)
    heat_offset, moist_offset, factor, exchange = (held[k:k + 1] for k in range(1, 5))

    share, flux, link, bottom = share_ref[...], flux_ref[...], link_ref[...], bottom_ref[...]
    temp = bottom
    for _ in range(SWEEPS):
        sat = 0.6 * jnp.exp(0.3 * temp)
        air_heat = heat_offset + factor * jnp.sum(share * temp, axis=0, keepdims=True)
        air_moist = moist_offset + factor * jnp.sum(share * sat, axis=0, keepdims=True)
        emitted = 0.5 * jnp.exp(0.2 * temp)
        residual = (
            flux
            - emitted
            - exchange * (temp - air_heat)
            - VAPOUR_ENTHALPY * exchange * (sat - air_moist)
            - link * (temp - bottom)
        )
        slope = 0.2 * emitted + exchange * (1.0 + VAPOUR_ENTHALPY * 0.3 * sat) + link
        temp = temp + residual / slope
    kelvin_ref[...] = temp
    answer = jnp.concatenate(
        [
            jnp.sum(share * temp, axis=0, keepdims=True),
            jnp.sum(share * (0.6 * jnp.exp(0.3 * temp)), axis=0, keepdims=True),
            drift_ref[...],
            jnp.zeros((WORDS - 4, n), jnp.float32),
        ],
        axis=0,
    )
    answer = jnp.concatenate([answer[:, b * LANES:(b + 1) * LANES] for b in range(blocks)], axis=0)
    spread = dot(jnp.concatenate(halves(answer), axis=1), jnp.concatenate([place, place], axis=0), NN)
    reply = jnp.zeros((WORDS, far * per_far), jnp.float32)
    for b in range(blocks):
        reply = reply + jnp.where(block == b, spread[b * WORDS:(b + 1) * WORDS], 0.0)
    for g in range(far):
        reply_ref[g] = reply[:, g * per_far:(g + 1) * per_far]


def finish_kernel(back_ref, slot_ref, off_ref, fac_ref, kelvin_ref, out_hbm, kelvin_hbm, out_ref, sems):
    levels, fields, n = off_ref.shape
    near, cap, width = back_ref.shape
    save_kelvin = pltpu.make_async_copy(kelvin_ref, kelvin_hbm, sems.at[0])
    save_kelvin.start()
    per_far = near * cap
    far = width // WORDS
    slot = slot_ref[...]
    row = slot // per_far
    place = one_hot(slot % per_far, per_far)
    back = back_ref[...].reshape(per_far, width).T
    spread = dot(jnp.concatenate(halves(back), axis=1), jnp.concatenate([place, place], axis=0), NN)
    level = jnp.zeros((WORDS, n), jnp.float32)
    for g in range(far):
        level = level + jnp.where(row == g, spread[g * WORDS:(g + 1) * WORDS], 0.0)
    level = level[0:fields]
    saves = []
    step = levels // PIECES
    for k in range(levels - 1, -1, -1):
        level = off_ref[k] + fac_ref[k] * level
        out_ref[k] = level
        if k % step == 0:
            part = pl.ds(k, step)
            save = pltpu.make_async_copy(out_ref.at[part], out_hbm.at[part], sems.at[1 + k // step])
            save.start()
            saves.append(save)
    for save in saves:
        save.wait()
    save_kelvin.wait()


def call(kernel, out_shape, in_space, out_spaces, scratch, *args):
    if in_space == pltpu.HBM:
        args = [pltpu.with_memory_space_constraint(x, pltpu.HBM) for x in args]
    return pl.pallas_call(
        kernel,
        out_shape=out_shape,
        in_specs=[pl.BlockSpec(memory_space=in_space)] * len(args),
        out_specs=[pl.BlockSpec(memory_space=space) for space in out_spaces],
        scratch_shapes=scratch,
        compiler_params=pltpu.CompilerParams(vmem_limit_bytes=32 * 1024 * 1024),
    )(*args)


def exchange_parcels(parcels, near):
    far, words, _ = parcels.shape
    parcels = lax.all_to_all(parcels, "gx", split_axis=0, concat_axis=0, tiled=True)
    parcels = parcels.reshape(far * words, near * CAP).T.reshape(near, CAP, far * words)
    return lax.all_to_all(parcels, ("gy", "sa"), split_axis=0, concat_axis=0, tiled=True)


def per_device(profile, coefficients, owner, fractions, flags, flux, links, bottom, drift):
    far = lax.axis_size("gx")
    near = lax.axis_size(("gy", "sa"))
    n = profile.shape[2]
    f32, i32 = jnp.float32, jnp.int32
    shape = jax.ShapeDtypeStruct
    like = lambda x: shape(x.shape, x.dtype)
    held = lambda x: pltpu.VMEM(x.shape, x.dtype)
    vmem, hbm = pltpu.VMEM, pltpu.HBM
    offsets, factors, send, slot, share, flux, links, bottom, drift = call(
        lambda *refs: columns_kernel(far, near, *refs),
        [
            like(profile),
            like(profile),
            shape((far, WORDS, near * CAP), f32),
            shape((1, n), i32),
            like(fractions),
            like(flux),
            like(links),
            like(bottom),
            like(drift),
        ],
        hbm,
        [vmem] * 9,
        [held(x) for x in (profile, coefficients, owner, fractions, flags)] + [pltpu.SemaphoreType.DMA((9,))],
        profile, coefficients, owner, fractions, flags, flux, links, bottom, drift,
    )
    got = exchange_parcels(send, near)
    kelvin, reply = call(
        cells_kernel,
        [like(bottom), shape((far, WORDS, near * CAP), f32)],
        vmem,
        [vmem] * 2,
        [],
        got, share, flux, links, bottom, drift,
    )
    back = exchange_parcels(reply, near)
    advanced, kelvin = call(
        finish_kernel,
        [like(profile), like(bottom)],
        vmem,
        [hbm] * 2,
        [held(profile), pltpu.SemaphoreType.DMA((1 + PIECES,))],
        back, slot, offsets, factors, kelvin,
    )
    return advanced, kelvin


def solution(mesh):
    spread3 = P(None, None, ("gx", "gy", "sa"))
    spread2 = P(None, ("gx", "gy", "sa"))
    return jax.shard_map(
        per_device,
        mesh=mesh,
        in_specs=(spread3, spread3) + (spread2,) * 7,
        out_specs=(spread3, spread2),
        check_vma=False,
    )
```

```python
import jax
import jax.numpy as jnp
from jax import lax
from jax.experimental import pallas as pl
from jax.experimental.pallas import tpu as pltpu
from jax.sharding import PartitionSpec as P

SWEEPS = 3
WORDS = 8
SENT = 5
ANSWERED = 4
CAP = 4
LANES = 128
PIECES = 4
INP = 1
VAPOUR_ENTHALPY = 2.5
NT = (((1,), (1,)), ((), ()))
NN = (((1,), (0,)), ((), ()))


def halves(x):
    high = x.astype(jnp.bfloat16)
    return high, (x - high.astype(jnp.float32)).astype(jnp.bfloat16)


def one_hot(index_row, count):
    ids = lax.broadcasted_iota(jnp.int32, (count, index_row.shape[1]), 0)
    return jnp.where(ids == index_row, 1.0, 0.0).astype(jnp.bfloat16)


def dot(a, b, dims):
    return lax.dot_general(a, b, dims, preferred_element_type=jnp.float32)


def columns_kernel(
    far,
    near,
    prof_hbm,
    coef_hbm,
    owner_hbm,
    fraction_hbm,
    flag_hbm,
    flux_hbm,
    link_hbm,
    bottom_hbm,
    drift_hbm,
    off_ref,
    fac_ref,
    send_ref,
    slot_ref,
    share_ref,
    flux_ref,
    link_ref,
    bottom_ref,
    drift_ref,
    prof_ref,
    coef_ref,
    owner_ref,
    fraction_ref,
    flag_ref,
    sems,
):
    levels, rows, _ = prof_ref.shape
    n = owner_ref.shape[1]
    blocks = n // LANES
    fields = rows // blocks
    step = levels // INP
    parts = [pl.ds(k * step, step) for k in range(INP)]
    pairs = [(owner_hbm, owner_ref)]
    for part in parts:
        pairs += [(coef_hbm.at[part], coef_ref.at[part]), (prof_hbm.at[part], prof_ref.at[part])]
    pairs += [
        (fraction_hbm, fraction_ref),
        (flag_hbm, flag_ref),
        (flux_hbm, flux_ref),
        (link_hbm, link_ref),
        (bottom_hbm, bottom_ref),
        (drift_hbm, drift_ref),
    ]
    copies = [pltpu.make_async_copy(a, b, sems.at[k]) for k, (a, b) in enumerate(pairs)]
    for copy in copies:
        copy.start()
    copies[0].wait()
    owner = owner_ref[0:1, :]
    tall = jnp.concatenate([owner[:, j * LANES:(j + 1) * LANES] for j in range(blocks)], axis=0).T
    earlier = lax.broadcasted_iota(jnp.int32, (LANES, LANES), 0) < lax.broadcasted_iota(jnp.int32, (LANES, LANES), 1)
    totals = [jnp.zeros((1, LANES), jnp.int32) for _ in range(blocks)]
    for i in range(blocks):
        source = jnp.broadcast_to(tall[:, i:i + 1], (LANES, LANES))
        for j in range(i, blocks):
            same = source == owner[:, j * LANES:(j + 1) * LANES]
            if i == j:
                same = same & earlier
            totals[j] += jnp.sum(same.astype(jnp.int32), axis=0, keepdims=True)
    slot = owner * CAP + jnp.concatenate(totals, axis=1)
    slot_ref[...] = slot
    per_far = near * CAP
    row = slot // per_far
    place = one_hot(slot % per_far, per_far)

    pair = lax.broadcasted_iota(jnp.int32, (8, LANES), 0) // 2
    above = last = before = shift = None
    for k in range(levels):
        if k % step == 0:
            copies[1 + 2 * (k // step)].wait()
            copies[2 + 2 * (k // step)].wait()
        below = jnp.concatenate(
            [
                jnp.take_along_axis(
                    coef_ref[k, 8 * (j // 2):8 * (j // 2) + 8], pair + 4 * (j % 2), axis=0, mode="promise_in_bounds"
                )
                for j in range(rows // 8)
            ],
            axis=0,
        )
        if k == 0:
            now, shift, numerator = 1.0 + below, prof_ref[k], below
        else:
            now = (1.0 + above + below) * last
            if k > 1:
                now = now - above * above * before
            else:
                now = now - above * above
            shift = prof_ref[k] * last + above * shift
            numerator = below * last
        inverse = 1.0 / now
        offset = shift * inverse
        factor = numerator * inverse
        off_ref[k] = offset
        fac_ref[k] = factor
        above, before, last = below, last, now

    values = []
    for t in range(blocks):
        at = fields * t
        code = (owner_ref[1:2, t * LANES:(t + 1) * LANES] + 1).astype(jnp.float32)
        values.append(
            jnp.concatenate(
                [offset[at:at + 2], factor[at:at + 1], below[at:at + 1], code, jnp.zeros((WORDS - 5, LANES), jnp.float32)],
                axis=0,
            )
        )
    values = jnp.concatenate(values, axis=1)
    spread = jnp.concatenate([jnp.where(row == g, values, 0.0) for g in range(far)], axis=0)
    sent = dot(jnp.concatenate(halves(spread), axis=0), place, NT)
    half = far * WORDS
    sent = sent[:half] + sent[half:]
    for g in range(far):
        send_ref[g] = sent[g * WORDS:g * WORDS + SENT]

    rest = copies[1 + 2 * INP:]
    rest[0].wait()
    rest[1].wait()
    water = fraction_ref[0:1, :]
    ice = fraction_ref[1:, :] * flag_ref[...].astype(jnp.float32)
    inverse = 1.0 / (water + jnp.sum(ice, axis=0, keepdims=True))
    share_ref[0:1, :] = water * inverse
    share_ref[1:, :] = ice * inverse
    for copy in rest[2:]:
        copy.wait()


def cells_kernel(got_ref, share_ref, flux_ref, link_ref, bottom_ref, drift_ref, kelvin_ref, reply_ref):
    far = reply_ref.shape[0]
    per_far = reply_ref.shape[2]
    n = share_ref.shape[1]
    blocks = n // LANES
    got = got_ref[...].reshape(per_far, far * WORDS).T
    got = jnp.concatenate([got[g * WORDS:(g + 1) * WORDS] for g in range(far)], axis=1)
    cell = got[4:5].astype(jnp.int32) - 1
    block = cell // LANES
    block = jnp.where(cell < 0, -1, block)
    place = one_hot(cell % LANES, LANES)
    spread = jnp.concatenate([jnp.where(block == b, got, 0.0) for b in range(blocks)], axis=0)
    rows = blocks * WORDS
    held = dot(jnp.concatenate(halves(spread), axis=0), place, NT)
    held = held[:rows] + held[rows:]
    held = jnp.concatenate([held[b * WORDS:(b + 1) * WORDS] for b in range(blocks)], axis=1)
    heat_offset, moist_offset, factor, exchange = (held[k:k + 1] for k in range(4))

    share, flux, link, bottom = share_ref[...], flux_ref[...], link_ref[...], bottom_ref[...]
    temp = bottom
    for _ in range(SWEEPS):
        sat = 0.6 * jnp.exp(0.3 * temp)
        air_heat = heat_offset + factor * jnp.sum(share * temp, axis=0, keepdims=True)
        air_moist = moist_offset + factor * jnp.sum(share * sat, axis=0, keepdims=True)
        emitted = 0.5 * jnp.exp(0.2 * temp)
        residual = (
            flux
            - emitted
            - exchange * (temp - air_heat)
            - VAPOUR_ENTHALPY * exchange * (sat - air_moist)
            - link * (temp - bottom)
        )
        slope = 0.2 * emitted + exchange * (1.0 + VAPOUR_ENTHALPY * 0.3 * sat) + link
        temp = temp + residual / slope
    kelvin_ref[...] = temp
    answer = jnp.concatenate(
        [
            jnp.sum(share * temp, axis=0, keepdims=True),
            jnp.sum(share * (0.6 * jnp.exp(0.3 * temp)), axis=0, keepdims=True),
            drift_ref[...],
            jnp.zeros((WORDS - 4, n), jnp.float32),
        ],
        axis=0,
    )
    answer = jnp.concatenate([answer[:, b * LANES:(b + 1) * LANES] for b in range(blocks)], axis=0)
    spread = dot(jnp.concatenate(halves(answer), axis=1), jnp.concatenate([place, place], axis=0), NN)
    reply = jnp.zeros((WORDS, far * per_far), jnp.float32)
    for b in range(blocks):
        reply = reply + jnp.where(block == b, spread[b * WORDS:(b + 1) * WORDS], 0.0)
    for g in range(far):
        reply_ref[g] = reply[0:ANSWERED, g * per_far:(g + 1) * per_far]


def finish_kernel(back_ref, slot_ref, off_ref, fac_ref, kelvin_ref, out_hbm, kelvin_hbm, out_ref, sems):
    levels, rows, _ = off_ref.shape
    n = slot_ref.shape[1]
    blocks = n // LANES
    fields = rows // blocks
    near, cap, width = back_ref.shape
    save_kelvin = pltpu.make_async_copy(kelvin_ref, kelvin_hbm, sems.at[0])
    save_kelvin.start()
    per_far = near * cap
    far = width // WORDS
    slot = slot_ref[...]
    row = slot // per_far
    place = one_hot(slot % per_far, per_far)
    back = back_ref[...].reshape(per_far, width).T
    spread = dot(jnp.concatenate(halves(back), axis=1), jnp.concatenate([place, place], axis=0), NN)
    level = jnp.zeros((WORDS, n), jnp.float32)
    for g in range(far):
        level = level + jnp.where(row == g, spread[g * WORDS:(g + 1) * WORDS], 0.0)
    level = jnp.concatenate([level[0:fields, t * LANES:(t + 1) * LANES] for t in range(blocks)], axis=0)
    saves = []
    step = levels // PIECES
    for k in range(levels - 1, -1, -1):
        level = off_ref[k] + fac_ref[k] * level
        out_ref[k] = level
        if k % step == 0:
            part = pl.ds(k, step)
            save = pltpu.make_async_copy(out_ref.at[part], out_hbm.at[part], sems.at[1 + k // step])
            save.start()
            saves.append(save)
    for save in saves:
        save.wait()
    save_kelvin.wait()


def call(kernel, out_shape, in_space, out_spaces, scratch, *args):
    if in_space == pltpu.HBM:
        args = [pltpu.with_memory_space_constraint(x, pltpu.HBM) for x in args]
    return pl.pallas_call(
        kernel,
        out_shape=out_shape,
        in_specs=[pl.BlockSpec(memory_space=in_space)] * len(args),
        out_specs=[pl.BlockSpec(memory_space=space) for space in out_spaces],
        scratch_shapes=scratch,
        compiler_params=pltpu.CompilerParams(vmem_limit_bytes=32 * 1024 * 1024),
    )(*args)


def exchange_parcels(parcels, near):
    far, words, _ = parcels.shape
    parcels = lax.all_to_all(parcels, "gx", split_axis=0, concat_axis=0, tiled=True)
    parcels = jnp.pad(parcels, ((0, 0), (0, WORDS - words), (0, 0)))
    parcels = parcels.reshape(far * WORDS, near * CAP).T.reshape(near, CAP, far * WORDS)
    return lax.all_to_all(parcels, ("gy", "sa"), split_axis=0, concat_axis=0, tiled=True)


def blocked(x):
    levels, fields, n = x.shape
    x = x.reshape(levels, fields, n // LANES, LANES).transpose(0, 2, 1, 3)
    return x.reshape(levels, fields * n // LANES, LANES)


def unblocked(x, fields):
    levels, rows, _ = x.shape
    x = x.reshape(levels, rows // fields, fields, LANES).transpose(0, 2, 1, 3)
    return x.reshape(levels, fields, rows * LANES // fields)


def per_device(profile, coefficients, owner, fractions, flags, flux, links, bottom, drift):
    far = lax.axis_size("gx")
    near = lax.axis_size(("gy", "sa"))
    fields, n = profile.shape[1:]
    profile, coefficients = blocked(profile), blocked(coefficients)
    f32, i32 = jnp.float32, jnp.int32
    shape = jax.ShapeDtypeStruct
    like = lambda x: shape(x.shape, x.dtype)
    held = lambda x: pltpu.VMEM(x.shape, x.dtype)
    vmem, hbm = pltpu.VMEM, pltpu.HBM
    offsets, factors, send, slot, share, flux, links, bottom, drift = call(
        lambda *refs: columns_kernel(far, near, *refs),
        [
            like(profile),
            like(profile),
            shape((far, SENT, near * CAP), f32),
            shape((1, n), i32),
            like(fractions),
            like(flux),
            like(links),
            like(bottom),
            like(drift),
        ],
        hbm,
        [vmem] * 9,
        [held(x) for x in (profile, coefficients, owner, fractions, flags)] + [pltpu.SemaphoreType.DMA((7 + 2 * INP,))],
        profile, coefficients, owner, fractions, flags, flux, links, bottom, drift,
    )
    got = exchange_parcels(send, near)
    kelvin, reply = call(
        cells_kernel,
        [like(bottom), shape((far, ANSWERED, near * CAP), f32)],
        vmem,
        [vmem] * 2,
        [],
        got, share, flux, links, bottom, drift,
    )
    back = exchange_parcels(reply, near)
    advanced, kelvin = call(
        finish_kernel,
        [like(profile), like(bottom)],
        vmem,
        [hbm] * 2,
        [held(profile), pltpu.SemaphoreType.DMA((1 + PIECES,))],
        back, slot, offsets, factors, kelvin,
    )
    return unblocked(advanced, fields), kelvin


def solution(mesh):
    spread3 = P(None, None, ("gx", "gy", "sa"))
    spread2 = P(None, ("gx", "gy", "sa"))
    return jax.shard_map(
        per_device,
        mesh=mesh,
        in_specs=(spread3, spread3) + (spread2,) * 7,
        out_specs=(spread3, spread2),
        check_vma=False,
    )
```

```python
import jax
import jax.numpy as jnp
from jax import lax
from jax.experimental import pallas as pl
from jax.experimental.pallas import tpu as pltpu
from jax.sharding import PartitionSpec as P

SWEEPS = 3
FAR_FIRST = (8, 8)
NEAR_FIRST = (22, 22)
WORDS = 8
SENT = 5
ANSWERED = 4
CAP = 4
LANES = 128
PIECES = 4
INP = 1
VAPOUR_ENTHALPY = 2.5
NT = (((1,), (1,)), ((), ()))
NN = (((1,), (0,)), ((), ()))


def halves(x):
    high = x.astype(jnp.bfloat16)
    return high, (x - high.astype(jnp.float32)).astype(jnp.bfloat16)


def one_hot(index_row, count):
    ids = lax.broadcasted_iota(jnp.int32, (count, index_row.shape[1]), 0)
    return jnp.where(ids == index_row, 1.0, 0.0).astype(jnp.bfloat16)


def dot(a, b, dims):
    return lax.dot_general(a, b, dims, preferred_element_type=jnp.float32)


def columns_kernel(
    far,
    near,
    prof_hbm,
    coef_hbm,
    owner_hbm,
    fraction_hbm,
    flag_hbm,
    flux_hbm,
    link_hbm,
    bottom_hbm,
    drift_hbm,
    off_ref,
    fac_ref,
    send_ref,
    slot_ref,
    share_ref,
    flux_ref,
    link_ref,
    bottom_ref,
    drift_ref,
    prof_ref,
    coef_ref,
    owner_ref,
    fraction_ref,
    flag_ref,
    sems,
):
    levels, rows, _ = prof_ref.shape
    n = owner_ref.shape[1]
    blocks = n // LANES
    fields = rows // blocks
    step = levels // INP
    parts = [pl.ds(k * step, step) for k in range(INP)]
    pairs = [(owner_hbm, owner_ref)]
    for part in parts:
        pairs += [(coef_hbm.at[part], coef_ref.at[part]), (prof_hbm.at[part], prof_ref.at[part])]
    pairs += [
        (fraction_hbm, fraction_ref),
        (flag_hbm, flag_ref),
        (flux_hbm, flux_ref),
        (link_hbm, link_ref),
        (bottom_hbm, bottom_ref),
        (drift_hbm, drift_ref),
    ]
    copies = [pltpu.make_async_copy(a, b, sems.at[k]) for k, (a, b) in enumerate(pairs)]
    for copy in copies:
        copy.start()
    copies[0].wait()
    owner = owner_ref[0:1, :]
    tall = jnp.concatenate([owner[:, j * LANES:(j + 1) * LANES] for j in range(blocks)], axis=0).T
    earlier = lax.broadcasted_iota(jnp.int32, (LANES, LANES), 0) < lax.broadcasted_iota(jnp.int32, (LANES, LANES), 1)
    totals = [jnp.zeros((1, LANES), jnp.int32) for _ in range(blocks)]
    for i in range(blocks):
        source = jnp.broadcast_to(tall[:, i:i + 1], (LANES, LANES))
        for j in range(i, blocks):
            same = source == owner[:, j * LANES:(j + 1) * LANES]
            if i == j:
                same = same & earlier
            totals[j] += jnp.sum(same.astype(jnp.int32), axis=0, keepdims=True)
    per_far = near * CAP
    row = (owner // near + (far - FAR_FIRST[0])) % far
    lane = (owner % near + (near - NEAR_FIRST[0])) % near * CAP + jnp.concatenate(totals, axis=1)
    slot_ref[0:1] = row
    slot_ref[1:2] = lane
    place = one_hot(lane, per_far)

    pair = lax.broadcasted_iota(jnp.int32, (8, LANES), 0) // 2
    above = last = before = shift = None
    for k in range(levels):
        if k % step == 0:
            copies[1 + 2 * (k // step)].wait()
            copies[2 + 2 * (k // step)].wait()
        below = jnp.concatenate(
            [
                jnp.take_along_axis(
                    coef_ref[k, 8 * (j // 2):8 * (j // 2) + 8], pair + 4 * (j % 2), axis=0, mode="promise_in_bounds"
                )
                for j in range(rows // 8)
            ],
            axis=0,
        )
        if k == 0:
            now, shift, numerator = 1.0 + below, prof_ref[k], below
        else:
            now = (1.0 + above + below) * last
            if k > 1:
                now = now - above * above * before
            else:
                now = now - above * above
            shift = prof_ref[k] * last + above * shift
            numerator = below * last
        inverse = 1.0 / now
        offset = shift * inverse
        factor = numerator * inverse
        off_ref[k] = offset
        fac_ref[k] = factor
        above, before, last = below, last, now

    values = []
    for t in range(blocks):
        at = fields * t
        code = (owner_ref[1:2, t * LANES:(t + 1) * LANES] + 1).astype(jnp.float32)
        values.append(
            jnp.concatenate(
                [offset[at:at + 2], factor[at:at + 1], below[at:at + 1], code, jnp.zeros((WORDS - 5, LANES), jnp.float32)],
                axis=0,
            )
        )
    values = jnp.concatenate(values, axis=1)
    spread = jnp.concatenate([jnp.where(row == g, values, 0.0) for g in range(far)], axis=0)
    sent = dot(jnp.concatenate(halves(spread), axis=0), place, NT)
    half = far * WORDS
    sent = sent[:half] + sent[half:]
    for g in range(far):
        send_ref[g] = sent[g * WORDS:g * WORDS + SENT]

    rest = copies[1 + 2 * INP:]
    rest[0].wait()
    rest[1].wait()
    water = fraction_ref[0:1, :]
    ice = fraction_ref[1:, :] * flag_ref[...].astype(jnp.float32)
    inverse = 1.0 / (water + jnp.sum(ice, axis=0, keepdims=True))
    share_ref[0:1, :] = water * inverse
    share_ref[1:, :] = ice * inverse
    for copy in rest[2:]:
        copy.wait()


def cells_kernel(got_ref, share_ref, flux_ref, link_ref, bottom_ref, drift_ref, kelvin_ref, reply_ref):
    far = reply_ref.shape[0]
    per_far = reply_ref.shape[2]
    n = share_ref.shape[1]
    blocks = n // LANES
    got = got_ref[...].reshape(per_far, far * WORDS).T
    got = jnp.concatenate([got[g * WORDS:(g + 1) * WORDS] for g in range(far)], axis=1)
    cell = got[4:5].astype(jnp.int32) - 1
    block = cell // LANES
    block = jnp.where(cell < 0, -1, block)
    place = one_hot(cell % LANES, LANES)
    spread = jnp.concatenate([jnp.where(block == b, got, 0.0) for b in range(blocks)], axis=0)
    rows = blocks * WORDS
    held = dot(jnp.concatenate(halves(spread), axis=0), place, NT)
    held = held[:rows] + held[rows:]
    held = jnp.concatenate([held[b * WORDS:(b + 1) * WORDS] for b in range(blocks)], axis=1)
    heat_offset, moist_offset, factor, exchange = (held[k:k + 1] for k in range(4))

    share, flux, link, bottom = share_ref[...], flux_ref[...], link_ref[...], bottom_ref[...]
    temp = bottom
    for _ in range(SWEEPS):
        sat = 0.6 * jnp.exp(0.3 * temp)
        air_heat = heat_offset + factor * jnp.sum(share * temp, axis=0, keepdims=True)
        air_moist = moist_offset + factor * jnp.sum(share * sat, axis=0, keepdims=True)
        emitted = 0.5 * jnp.exp(0.2 * temp)
        residual = (
            flux
            - emitted
            - exchange * (temp - air_heat)
            - VAPOUR_ENTHALPY * exchange * (sat - air_moist)
            - link * (temp - bottom)
        )
        slope = 0.2 * emitted + exchange * (1.0 + VAPOUR_ENTHALPY * 0.3 * sat) + link
        temp = temp + residual / slope
    kelvin_ref[...] = temp
    answer = jnp.concatenate(
        [
            jnp.sum(share * temp, axis=0, keepdims=True),
            jnp.sum(share * (0.6 * jnp.exp(0.3 * temp)), axis=0, keepdims=True),
            drift_ref[...],
            jnp.zeros((WORDS - 4, n), jnp.float32),
        ],
        axis=0,
    )
    answer = jnp.concatenate([answer[:, b * LANES:(b + 1) * LANES] for b in range(blocks)], axis=0)
    spread = dot(jnp.concatenate(halves(answer), axis=1), jnp.concatenate([place, place], axis=0), NN)
    shift = (NEAR_FIRST[0] - NEAR_FIRST[1]) * CAP % per_far
    reply = jnp.zeros((WORDS, far * per_far), jnp.float32)
    for b in range(blocks):
        reply = reply + jnp.where(block == b, spread[b * WORDS:(b + 1) * WORDS], 0.0)
    for g in range(far):
        part = reply[0:ANSWERED, g * per_far:(g + 1) * per_far]
        if shift:
            part = jnp.concatenate([part[:, per_far - shift:], part[:, :per_far - shift]], axis=1)
        reply_ref[(g + FAR_FIRST[0] - FAR_FIRST[1]) % far] = part


def finish_kernel(back_ref, slot_ref, off_ref, fac_ref, kelvin_ref, out_hbm, kelvin_hbm, out_ref, sems):
    levels, rows, _ = off_ref.shape
    n = slot_ref.shape[1]
    blocks = n // LANES
    fields = rows // blocks
    near, cap, width = back_ref.shape
    save_kelvin = pltpu.make_async_copy(kelvin_ref, kelvin_hbm, sems.at[0])
    save_kelvin.start()
    per_far = near * cap
    far = width // WORDS
    row = (slot_ref[0:1] + (far + FAR_FIRST[0] - FAR_FIRST[1])) % far
    shift = (NEAR_FIRST[0] - NEAR_FIRST[1]) * CAP % per_far
    place = one_hot((slot_ref[1:2] + shift) % per_far, per_far)
    back = back_ref[...].reshape(per_far, width).T
    spread = dot(jnp.concatenate(halves(back), axis=1), jnp.concatenate([place, place], axis=0), NN)
    level = jnp.zeros((WORDS, n), jnp.float32)
    for g in range(far):
        level = level + jnp.where(row == g, spread[g * WORDS:(g + 1) * WORDS], 0.0)
    level = jnp.concatenate([level[0:fields, t * LANES:(t + 1) * LANES] for t in range(blocks)], axis=0)
    saves = []
    step = levels // PIECES
    for k in range(levels - 1, -1, -1):
        level = off_ref[k] + fac_ref[k] * level
        out_ref[k] = level
        if k % step == 0:
            part = pl.ds(k, step)
            save = pltpu.make_async_copy(out_ref.at[part], out_hbm.at[part], sems.at[1 + k // step])
            save.start()
            saves.append(save)
    for save in saves:
        save.wait()
    save_kelvin.wait()


def call(kernel, out_shape, in_space, out_spaces, scratch, *args):
    if in_space == pltpu.HBM:
        args = [pltpu.with_memory_space_constraint(x, pltpu.HBM) for x in args]
    return pl.pallas_call(
        kernel,
        out_shape=out_shape,
        in_specs=[pl.BlockSpec(memory_space=in_space)] * len(args),
        out_specs=[pl.BlockSpec(memory_space=space) for space in out_spaces],
        scratch_shapes=scratch,
        compiler_params=pltpu.CompilerParams(vmem_limit_bytes=32 * 1024 * 1024),
    )(*args)


def exchange_parcels(parcels, near, far_first, near_first):
    far, words, _ = parcels.shape
    axes = ("gx", "gy", "sa")
    far_order = [(k + far_first) % far for k in range(far)]
    near_order = [(k + near_first) % near for k in range(near)]
    far_groups = [[f * near + q for f in far_order] for q in range(near)]
    near_groups = [[f * near + q for q in near_order] for f in range(far)]
    parcels = lax.all_to_all(parcels, axes, 0, 0, axis_index_groups=far_groups, tiled=True)
    parcels = jnp.pad(parcels, ((0, 0), (0, WORDS - words), (0, 0)))
    parcels = parcels.reshape(far * WORDS, near * CAP).T.reshape(near, CAP, far * WORDS)
    return lax.all_to_all(parcels, axes, 0, 0, axis_index_groups=near_groups, tiled=True)


def blocked(x):
    levels, fields, n = x.shape
    x = x.reshape(levels, fields, n // LANES, LANES).transpose(0, 2, 1, 3)
    return x.reshape(levels, fields * n // LANES, LANES)


def unblocked(x, fields):
    levels, rows, _ = x.shape
    x = x.reshape(levels, rows // fields, fields, LANES).transpose(0, 2, 1, 3)
    return x.reshape(levels, fields, rows * LANES // fields)


def per_device(profile, coefficients, owner, fractions, flags, flux, links, bottom, drift):
    far = lax.axis_size("gx")
    near = lax.axis_size(("gy", "sa"))
    fields, n = profile.shape[1:]
    profile, coefficients = blocked(profile), blocked(coefficients)
    f32, i32 = jnp.float32, jnp.int32
    shape = jax.ShapeDtypeStruct
    like = lambda x: shape(x.shape, x.dtype)
    held = lambda x: pltpu.VMEM(x.shape, x.dtype)
    vmem, hbm = pltpu.VMEM, pltpu.HBM
    offsets, factors, send, slot, share, flux, links, bottom, drift = call(
        lambda *refs: columns_kernel(far, near, *refs),
        [
            like(profile),
            like(profile),
            shape((far, SENT, near * CAP), f32),
            shape((2, n), i32),
            like(fractions),
            like(flux),
            like(links),
            like(bottom),
            like(drift),
        ],
        hbm,
        [vmem] * 9,
        [held(x) for x in (profile, coefficients, owner, fractions, flags)] + [pltpu.SemaphoreType.DMA((7 + 2 * INP,))],
        profile, coefficients, owner, fractions, flags, flux, links, bottom, drift,
    )
    got = exchange_parcels(send, near, FAR_FIRST[0], NEAR_FIRST[0])
    kelvin, reply = call(
        cells_kernel,
        [like(bottom), shape((far, ANSWERED, near * CAP), f32)],
        vmem,
        [vmem] * 2,
        [],
        got, share, flux, links, bottom, drift,
    )
    back = exchange_parcels(reply, near, FAR_FIRST[1], NEAR_FIRST[1])
    advanced, kelvin = call(
        finish_kernel,
        [like(profile), like(bottom)],
        vmem,
        [hbm] * 2,
        [held(profile), pltpu.SemaphoreType.DMA((1 + PIECES,))],
        back, slot, offsets, factors, kelvin,
    )
    return unblocked(advanced, fields), kelvin


def solution(mesh):
    spread3 = P(None, None, ("gx", "gy", "sa"))
    spread2 = P(None, ("gx", "gy", "sa"))
    return jax.shard_map(
        per_device,
        mesh=mesh,
        in_specs=(spread3, spread3) + (spread2,) * 7,
        out_specs=(spread3, spread2),
        check_vma=False,
    )
```

```python
import jax
import jax.numpy as jnp
from jax import lax
from jax.experimental import pallas as pl
from jax.experimental.pallas import tpu as pltpu
from jax.sharding import PartitionSpec as P

SWEEPS = 3
FAR_FIRST = (8, 8)
NEAR_FIRST = (22, 22)
WORDS = 8
SENT = 5
ANSWERED = 4
CAP = 4
LANES = 128
PIECES = 4
INP = 1
VAPOUR_ENTHALPY = 2.5
NT = (((1,), (1,)), ((), ()))
NN = (((1,), (0,)), ((), ()))


def halves(x):
    high = x.astype(jnp.bfloat16)
    return high, (x - high.astype(jnp.float32)).astype(jnp.bfloat16)


def stacked_halves(x):
    high = x.astype(jnp.bfloat16).astype(jnp.float32)
    return jnp.concatenate([high, x - high], axis=0)


def one_hot(index_row, count):
    ids = lax.broadcasted_iota(jnp.int32, (count, index_row.shape[1]), 0)
    return jnp.where(ids == index_row, 1.0, 0.0).astype(jnp.bfloat16)


def dot(a, b, dims):
    return lax.dot_general(a, b, dims, preferred_element_type=jnp.float32)


def columns_kernel(
    far,
    near,
    prof_hbm,
    coef_hbm,
    owner_hbm,
    fraction_hbm,
    flag_hbm,
    flux_hbm,
    link_hbm,
    bottom_hbm,
    drift_hbm,
    off_ref,
    fac_ref,
    send_ref,
    slot_ref,
    share_ref,
    base_ref,
    link_ref,
    bottom_ref,
    drift_ref,
    prof_ref,
    coef_ref,
    owner_ref,
    fraction_ref,
    flag_ref,
    flux_in,
    link_in,
    bottom_in,
    drift_in,
    sems,
):
    levels, rows, _ = prof_ref.shape
    n = owner_ref.shape[1]
    blocks = n // LANES
    fields = rows // blocks
    step = levels // INP
    parts = [pl.ds(k * step, step) for k in range(INP)]
    pairs = [(owner_hbm, owner_ref)]
    for part in parts:
        pairs += [(coef_hbm.at[part], coef_ref.at[part]), (prof_hbm.at[part], prof_ref.at[part])]
    pairs += [
        (fraction_hbm, fraction_ref),
        (flag_hbm, flag_ref),
        (flux_hbm, flux_in),
        (link_hbm, link_in),
        (bottom_hbm, bottom_in),
        (drift_hbm, drift_in),
    ]
    copies = [pltpu.make_async_copy(a, b, sems.at[k]) for k, (a, b) in enumerate(pairs)]
    for copy in copies:
        copy.start()
    copies[0].wait()
    owner = owner_ref[0:1, :]
    tall = jnp.concatenate([owner[:, j * LANES:(j + 1) * LANES] for j in range(blocks)], axis=0).T
    earlier = lax.broadcasted_iota(jnp.int32, (LANES, LANES), 0) < lax.broadcasted_iota(jnp.int32, (LANES, LANES), 1)
    totals = [jnp.zeros((1, LANES), jnp.int32) for _ in range(blocks)]
    for i in range(blocks):
        source = jnp.broadcast_to(tall[:, i:i + 1], (LANES, LANES))
        for j in range(i, blocks):
            same = source == owner[:, j * LANES:(j + 1) * LANES]
            if i == j:
                same = same & earlier
            totals[j] += jnp.sum(same.astype(jnp.int32), axis=0, keepdims=True)
    per_far = near * CAP
    row = (owner // near + (far - FAR_FIRST[0])) % far
    lane = (owner % near + (near - NEAR_FIRST[0])) % near * CAP + jnp.concatenate(totals, axis=1)
    slot_ref[0:1] = row
    slot_ref[1:2] = lane
    place = one_hot(lane, per_far)

    pair = lax.broadcasted_iota(jnp.int32, (8, LANES), 0) // 2
    above = last = before = shift = None
    for k in range(levels):
        if k % step == 0:
            copies[1 + 2 * (k // step)].wait()
            copies[2 + 2 * (k // step)].wait()
        below = jnp.concatenate(
            [
                jnp.take_along_axis(
                    coef_ref[k, 8 * (j // 2):8 * (j // 2) + 8], pair + 4 * (j % 2), axis=0, mode="promise_in_bounds"
                )
                for j in range(rows // 8)
            ],
            axis=0,
        )
        if k == 0:
            now, shift, numerator = 1.0 + below, prof_ref[k], below
        else:
            now = (1.0 + above + below) * last
            if k > 1:
                now = now - above * above * before
            else:
                now = now - above * above
            shift = prof_ref[k] * last + above * shift
            numerator = below * last
        inverse = 1.0 / now
        offset = shift * inverse
        factor = numerator * inverse
        off_ref[k] = offset
        fac_ref[k] = factor
        above, before, last = below, last, now

    values = []
    for t in range(blocks):
        at = fields * t
        code = (owner_ref[1:2, t * LANES:(t + 1) * LANES] + 1).astype(jnp.float32)
        values.append(
            jnp.concatenate(
                [offset[at:at + 2], factor[at:at + 1], below[at:at + 1], code, jnp.zeros((WORDS - 5, LANES), jnp.float32)],
                axis=0,
            )
        )
    values = stacked_halves(jnp.concatenate(values, axis=1))
    spread = jnp.concatenate([jnp.where(row == g, values, 0.0).astype(jnp.bfloat16) for g in range(far)], axis=0)
    sent = dot(spread, place, NT)
    for g in range(far):
        at = 2 * g * WORDS
        send_ref[g] = sent[at:at + SENT] + sent[at + WORDS:at + WORDS + SENT]

    rest = copies[1 + 2 * INP:]
    rest[0].wait()
    rest[1].wait()
    present = flag_ref[...].astype(jnp.float32)
    for t in range(blocks):
        part = slice(t * LANES, (t + 1) * LANES)
        share_ref[0:1, t] = fraction_ref[0:1, part]
        share_ref[1:, t] = fraction_ref[1:, part] * present[:, part]
    inverse = 1.0 / jnp.sum(share_ref[...], axis=0)
    for kind in range(share_ref.shape[0]):
        share_ref[kind] = share_ref[kind] * inverse
    for copy in rest[2:]:
        copy.wait()
    for t in range(blocks):
        part = slice(t * LANES, (t + 1) * LANES)
        link, bottom = link_in[:, part], bottom_in[:, part]
        base_ref[:, t] = flux_in[:, part] + link * bottom
        link_ref[:, t] = link
        bottom_ref[:, t] = bottom
        drift_ref[:, t] = drift_in[:, part]


def cells_kernel(got_ref, share_ref, base_ref, link_ref, bottom_ref, drift_ref, kelvin_ref, reply_ref, answer_ref):
    far = reply_ref.shape[0]
    per_far = reply_ref.shape[2]
    kinds, blocks, _ = share_ref.shape
    got = got_ref[...].reshape(per_far, far * WORDS).T
    high = got.astype(jnp.bfloat16).astype(jnp.float32)
    low = got - high
    word = lambda x, w: jnp.concatenate([x[g * WORDS + w:g * WORDS + w + 1] for g in range(far)], axis=1)
    cell = word(got, 4).astype(jnp.int32) - 1
    block = jnp.where(cell < 0, -1, cell // LANES)
    place = one_hot(cell % LANES, LANES)
    own = lax.broadcasted_iota(jnp.int32, (blocks, far * per_far), 0) == block
    spread = [jnp.where(own, word(x, w), 0.0) for w in range(4) for x in (high, low)]
    held = dot(jnp.concatenate(spread, axis=0).astype(jnp.bfloat16), place, NT)
    heat_offset, moist_offset, factor, exchange = (
        held[2 * w * blocks:(2 * w + 1) * blocks] + held[(2 * w + 1) * blocks:(2 * w + 2) * blocks] for w in range(4)
    )

    share = [share_ref[k] for k in range(kinds)]
    bottom = [bottom_ref[k] for k in range(kinds)]
    moist_pull = VAPOUR_ENTHALPY * exchange
    column_part = exchange * heat_offset + moist_pull * moist_offset
    heat_mix, moist_mix = exchange * factor, moist_pull * factor
    base = [base_ref[k] + column_part for k in range(kinds)]
    pull = [link_ref[k] + exchange for k in range(kinds)]
    temp = bottom
    for _ in range(SWEEPS):
        sat = [0.6 * jnp.exp(0.3 * t) for t in temp]
        emitted = [0.5 * jnp.exp(0.2 * t) for t in temp]
        mixed = heat_mix * sum(a * t for a, t in zip(share, temp)) + moist_mix * sum(a * q for a, q in zip(share, sat))
        for k in range(kinds):
            residual = (base[k] + mixed) - emitted[k] - pull[k] * temp[k] - moist_pull * sat[k]
            slope = 0.2 * emitted[k] + (0.3 * moist_pull) * sat[k] + pull[k]
            temp = temp[:k] + [temp[k] + residual / slope] + temp[k + 1:]
    for k in range(kinds):
        kelvin_ref[k] = temp[k]
    answers = (
        sum(a * t for a, t in zip(share, temp)),
        sum(a * (0.6 * jnp.exp(0.3 * t)) for a, t in zip(share, temp)),
        drift_ref[0],
        drift_ref[1],
    )
    for w, answer in enumerate(answers):
        answer_ref[pl.ds(w, blocks, stride=ANSWERED)] = answer
    spread = dot(
        jnp.concatenate(halves(answer_ref[...]), axis=1), jnp.concatenate([place, place], axis=0), NN
    )
    two = 2 * ANSWERED
    first = lax.broadcasted_iota(jnp.int32, (two, far * per_far), 0) // ANSWERED
    reply = jnp.zeros((two, far * per_far), jnp.float32)
    for b in range(0, blocks, 2):
        reply = reply + jnp.where(first == block - b, spread[b * ANSWERED:b * ANSWERED + two], 0.0)
    reply = reply[:ANSWERED] + reply[ANSWERED:]
    shift = (NEAR_FIRST[0] - NEAR_FIRST[1]) * CAP % per_far
    for g in range(far):
        part = reply[:, g * per_far:(g + 1) * per_far]
        if shift:
            part = jnp.concatenate([part[:, per_far - shift:], part[:, :per_far - shift]], axis=1)
        reply_ref[(g + FAR_FIRST[0] - FAR_FIRST[1]) % far] = part


def finish_kernel(back_ref, slot_ref, off_ref, fac_ref, kelvin_ref, out_hbm, kelvin_hbm, out_ref, flat_ref, sems):
    levels, rows, _ = off_ref.shape
    n = slot_ref.shape[1]
    blocks = n // LANES
    fields = rows // blocks
    near, cap, width = back_ref.shape
    for t in range(blocks):
        flat_ref[:, t * LANES:(t + 1) * LANES] = kelvin_ref[:, t]
    save_kelvin = pltpu.make_async_copy(flat_ref, kelvin_hbm, sems.at[0])
    save_kelvin.start()
    per_far = near * cap
    far = width // WORDS
    row = (slot_ref[0:1] + (far + FAR_FIRST[0] - FAR_FIRST[1])) % far
    shift = (NEAR_FIRST[0] - NEAR_FIRST[1]) * CAP % per_far
    place = one_hot((slot_ref[1:2] + shift) % per_far, per_far)
    back = back_ref[...].reshape(per_far, width).T
    spread = dot(jnp.concatenate(halves(back), axis=1), jnp.concatenate([place, place], axis=0), NN)
    level = jnp.zeros((WORDS, n), jnp.float32)
    for g in range(far):
        level = level + jnp.where(row == g, spread[g * WORDS:(g + 1) * WORDS], 0.0)
    level = jnp.concatenate([level[0:fields, t * LANES:(t + 1) * LANES] for t in range(blocks)], axis=0)
    saves = []
    step = levels // PIECES
    for k in range(levels - 1, -1, -1):
        level = off_ref[k] + fac_ref[k] * level
        out_ref[k] = level
        if k % step == 0:
            part = pl.ds(k, step)
            save = pltpu.make_async_copy(out_ref.at[part], out_hbm.at[part], sems.at[1 + k // step])
            save.start()
            saves.append(save)
    for save in saves:
        save.wait()
    save_kelvin.wait()


def call(kernel, out_shape, in_space, out_spaces, scratch, *args):
    if in_space == pltpu.HBM:
        args = [pltpu.with_memory_space_constraint(x, pltpu.HBM) for x in args]
    return pl.pallas_call(
        kernel,
        out_shape=out_shape,
        in_specs=[pl.BlockSpec(memory_space=in_space)] * len(args),
        out_specs=[pl.BlockSpec(memory_space=space) for space in out_spaces],
        scratch_shapes=scratch,
        compiler_params=pltpu.CompilerParams(vmem_limit_bytes=32 * 1024 * 1024),
    )(*args)


def exchange_parcels(parcels, near, far_first, near_first):
    far, words, _ = parcels.shape
    axes = ("gx", "gy", "sa")
    far_order = [(k + far_first) % far for k in range(far)]
    near_order = [(k + near_first) % near for k in range(near)]
    far_groups = [[f * near + q for f in far_order] for q in range(near)]
    near_groups = [[f * near + q for q in near_order] for f in range(far)]
    parcels = lax.all_to_all(parcels, axes, 0, 0, axis_index_groups=far_groups, tiled=True)
    parcels = jnp.pad(parcels, ((0, 0), (0, WORDS - words), (0, 0)))
    parcels = parcels.reshape(far * WORDS, near * CAP).T.reshape(near, CAP, far * WORDS)
    return lax.all_to_all(parcels, axes, 0, 0, axis_index_groups=near_groups, tiled=True)


def blocked(x):
    levels, fields, n = x.shape
    x = x.reshape(levels, fields, n // LANES, LANES).transpose(0, 2, 1, 3)
    return x.reshape(levels, fields * n // LANES, LANES)


def unblocked(x, fields):
    levels, rows, _ = x.shape
    x = x.reshape(levels, rows // fields, fields, LANES).transpose(0, 2, 1, 3)
    return x.reshape(levels, fields, rows * LANES // fields)


def per_device(profile, coefficients, owner, fractions, flags, flux, links, bottom, drift):
    far = lax.axis_size("gx")
    near = lax.axis_size(("gy", "sa"))
    fields, n = profile.shape[1:]
    profile, coefficients = blocked(profile), blocked(coefficients)
    f32, i32 = jnp.float32, jnp.int32
    shape = jax.ShapeDtypeStruct
    like = lambda x: shape(x.shape, x.dtype)
    held = lambda x: pltpu.VMEM(x.shape, x.dtype)
    vmem, hbm = pltpu.VMEM, pltpu.HBM
    offsets, factors, send, slot, *cells = call(
        lambda *refs: columns_kernel(far, near, *refs),
        [
            like(profile),
            like(profile),
            shape((far, SENT, near * CAP), f32),
            shape((2, n), i32),
            *[shape((x.shape[0], n // LANES, LANES), f32) for x in (fractions, flux, links, bottom, drift)],
        ],
        hbm,
        [vmem] * 9,
        [held(x) for x in (profile, coefficients, owner, fractions, flags, flux, links, bottom, drift)]
        + [pltpu.SemaphoreType.DMA((7 + 2 * INP,))],
        profile, coefficients, owner, fractions, flags, flux, links, bottom, drift,
    )
    got = exchange_parcels(send, near, FAR_FIRST[0], NEAR_FIRST[0])
    kelvin, reply = call(
        cells_kernel,
        [like(cells[0]), shape((far, ANSWERED, near * CAP), f32)],
        vmem,
        [vmem] * 2,
        [pltpu.VMEM((ANSWERED * n // LANES, LANES), f32)],
        got, *cells,
    )
    back = exchange_parcels(reply, near, FAR_FIRST[1], NEAR_FIRST[1])
    advanced, kelvin = call(
        finish_kernel,
        [like(profile), like(bottom)],
        vmem,
        [hbm] * 2,
        [held(profile), held(bottom), pltpu.SemaphoreType.DMA((1 + PIECES,))],
        back, slot, offsets, factors, kelvin,
    )
    return unblocked(advanced, fields), kelvin


def solution(mesh):
    spread3 = P(None, None, ("gx", "gy", "sa"))
    spread2 = P(None, ("gx", "gy", "sa"))
    return jax.shard_map(
        per_device,
        mesh=mesh,
        in_specs=(spread3, spread3) + (spread2,) * 7,
        out_specs=(spread3, spread2),
        check_vma=False,
    )
```

```python
import jax
import jax.numpy as jnp
from jax import lax
from jax.experimental import pallas as pl
from jax.experimental.pallas import tpu as pltpu
from jax.sharding import PartitionSpec as P

SWEEPS = 3
FAR_FIRST = (8, 8)
NEAR_FIRST = 22
WORDS = 8
SENT = 5
ANSWERED = 4
CAP = 4
LANES = 128
PIECES = 4
INP = 1
VAPOUR_ENTHALPY = 2.5
NT = (((1,), (1,)), ((), ()))
NN = (((1,), (0,)), ((), ()))


def halves(x):
    high = x.astype(jnp.bfloat16)
    return high, (x - high.astype(jnp.float32)).astype(jnp.bfloat16)


def stacked_halves(x):
    high = x.astype(jnp.bfloat16).astype(jnp.float32)
    return jnp.concatenate([high, x - high], axis=0)


def one_hot(index_row, count):
    ids = lax.broadcasted_iota(jnp.int32, (count, index_row.shape[1]), 0)
    return jnp.where(ids == index_row, 1.0, 0.0).astype(jnp.bfloat16)


def dot(a, b, dims):
    return lax.dot_general(a, b, dims, preferred_element_type=jnp.float32)


def columns_kernel(
    far,
    near,
    prof_hbm,
    coef_hbm,
    owner_hbm,
    fraction_hbm,
    flag_hbm,
    flux_hbm,
    link_hbm,
    bottom_hbm,
    drift_hbm,
    off_ref,
    fac_ref,
    send_ref,
    slot_ref,
    share_ref,
    base_ref,
    link_ref,
    bottom_ref,
    drift_ref,
    prof_ref,
    coef_ref,
    owner_ref,
    fraction_ref,
    flag_ref,
    flux_in,
    link_in,
    bottom_in,
    drift_in,
    sems,
):
    levels, rows, _ = prof_ref.shape
    n = owner_ref.shape[1]
    blocks = n // LANES
    fields = rows // blocks
    step = levels // INP
    parts = [pl.ds(k * step, step) for k in range(INP)]
    pairs = [(owner_hbm, owner_ref)]
    for part in parts:
        pairs += [(coef_hbm.at[part], coef_ref.at[part]), (prof_hbm.at[part], prof_ref.at[part])]
    pairs += [
        (fraction_hbm, fraction_ref),
        (flag_hbm, flag_ref),
        (flux_hbm, flux_in),
        (link_hbm, link_in),
        (bottom_hbm, bottom_in),
        (drift_hbm, drift_in),
    ]
    copies = [pltpu.make_async_copy(a, b, sems.at[k]) for k, (a, b) in enumerate(pairs)]
    for copy in copies:
        copy.start()
    copies[0].wait()
    owner = owner_ref[0:1, :]
    tall = jnp.concatenate([owner[:, j * LANES:(j + 1) * LANES] for j in range(blocks)], axis=0).T
    earlier = lax.broadcasted_iota(jnp.int32, (LANES, LANES), 0) < lax.broadcasted_iota(jnp.int32, (LANES, LANES), 1)
    totals = [jnp.zeros((1, LANES), jnp.int32) for _ in range(blocks)]
    for i in range(blocks):
        source = jnp.broadcast_to(tall[:, i:i + 1], (LANES, LANES))
        for j in range(i, blocks):
            same = source == owner[:, j * LANES:(j + 1) * LANES]
            if i == j:
                same = same & earlier
            totals[j] += jnp.sum(same.astype(jnp.int32), axis=0, keepdims=True)
    per_far = near * CAP
    row = (owner // near + (far - FAR_FIRST[0])) % far
    lane = (owner % near + (near - NEAR_FIRST)) % near * CAP + jnp.concatenate(totals, axis=1)
    slot_ref[0:1] = row
    slot_ref[1:2] = lane
    place = one_hot(lane, per_far)

    pair = lax.broadcasted_iota(jnp.int32, (8, LANES), 0) // 2
    above = last = before = shift = None
    for k in range(levels):
        if k % step == 0:
            copies[1 + 2 * (k // step)].wait()
            copies[2 + 2 * (k // step)].wait()
        below = jnp.concatenate(
            [
                jnp.take_along_axis(
                    coef_ref[k, 8 * (j // 2):8 * (j // 2) + 8], pair + 4 * (j % 2), axis=0, mode="promise_in_bounds"
                )
                for j in range(rows // 8)
            ],
            axis=0,
        )
        if k == 0:
            now, shift, numerator = 1.0 + below, prof_ref[k], below
        else:
            now = (1.0 + above + below) * last
            if k > 1:
                now = now - above * above * before
            else:
                now = now - above * above
            shift = prof_ref[k] * last + above * shift
            numerator = below * last
        inverse = 1.0 / now
        offset = shift * inverse
        factor = numerator * inverse
        off_ref[k] = offset
        fac_ref[k] = factor
        above, before, last = below, last, now

    values = []
    for t in range(blocks):
        at = fields * t
        code = (owner_ref[1:2, t * LANES:(t + 1) * LANES] + 1).astype(jnp.float32)
        values.append(
            jnp.concatenate(
                [offset[at:at + 2], factor[at:at + 1], below[at:at + 1], code, jnp.zeros((WORDS - 5, LANES), jnp.float32)],
                axis=0,
            )
        )
    values = stacked_halves(jnp.concatenate(values, axis=1))
    spread = jnp.concatenate([jnp.where(row == g, values, 0.0).astype(jnp.bfloat16) for g in range(far)], axis=0)
    sent = dot(spread, place, NT)
    for g in range(far):
        at = 2 * g * WORDS
        send_ref[g] = sent[at:at + SENT] + sent[at + WORDS:at + WORDS + SENT]

    rest = copies[1 + 2 * INP:]
    rest[0].wait()
    rest[1].wait()
    present = flag_ref[...].astype(jnp.float32)
    for t in range(blocks):
        part = slice(t * LANES, (t + 1) * LANES)
        share_ref[0:1, t] = fraction_ref[0:1, part]
        share_ref[1:, t] = fraction_ref[1:, part] * present[:, part]
    inverse = 1.0 / jnp.sum(share_ref[...], axis=0)
    for kind in range(share_ref.shape[0]):
        share_ref[kind] = share_ref[kind] * inverse
    for copy in rest[2:]:
        copy.wait()
    for t in range(blocks):
        part = slice(t * LANES, (t + 1) * LANES)
        link, bottom = link_in[:, part], bottom_in[:, part]
        base_ref[:, t] = flux_in[:, part] + link * bottom
        link_ref[:, t] = link
        bottom_ref[:, t] = bottom
        drift_ref[:, t] = drift_in[:, part]


def cells_kernel(got_ref, share_ref, base_ref, link_ref, bottom_ref, drift_ref, kelvin_ref, reply_ref, answer_ref):
    near, cap, width = got_ref.shape
    per_far = near * cap
    far = width // WORDS
    kinds, blocks, _ = share_ref.shape
    got = got_ref[...].reshape(per_far, far * WORDS).T
    high = got.astype(jnp.bfloat16).astype(jnp.float32)
    low = got - high
    word = lambda x, w: jnp.concatenate([x[g * WORDS + w:g * WORDS + w + 1] for g in range(far)], axis=1)
    cell = word(got, 4).astype(jnp.int32) - 1
    block = jnp.where(cell < 0, -1, cell // LANES)
    place = one_hot(cell % LANES, LANES)
    own = lax.broadcasted_iota(jnp.int32, (blocks, far * per_far), 0) == block
    spread = [jnp.where(own, word(x, w), 0.0) for w in range(4) for x in (high, low)]
    held = dot(jnp.concatenate(spread, axis=0).astype(jnp.bfloat16), place, NT)
    heat_offset, moist_offset, factor, exchange = (
        held[2 * w * blocks:(2 * w + 1) * blocks] + held[(2 * w + 1) * blocks:(2 * w + 2) * blocks] for w in range(4)
    )

    share = [share_ref[k] for k in range(kinds)]
    bottom = [bottom_ref[k] for k in range(kinds)]
    moist_pull = VAPOUR_ENTHALPY * exchange
    column_part = exchange * heat_offset + moist_pull * moist_offset
    heat_mix, moist_mix = exchange * factor, moist_pull * factor
    base = [base_ref[k] + column_part for k in range(kinds)]
    pull = [link_ref[k] + exchange for k in range(kinds)]
    temp = bottom
    for _ in range(SWEEPS):
        sat = [0.6 * jnp.exp(0.3 * t) for t in temp]
        emitted = [0.5 * jnp.exp(0.2 * t) for t in temp]
        mixed = heat_mix * sum(a * t for a, t in zip(share, temp)) + moist_mix * sum(a * q for a, q in zip(share, sat))
        for k in range(kinds):
            residual = (base[k] + mixed) - emitted[k] - pull[k] * temp[k] - moist_pull * sat[k]
            slope = 0.2 * emitted[k] + (0.3 * moist_pull) * sat[k] + pull[k]
            temp = temp[:k] + [temp[k] + residual / slope] + temp[k + 1:]
    for k in range(kinds):
        kelvin_ref[k] = temp[k]
    answers = (
        sum(a * t for a, t in zip(share, temp)),
        sum(a * (0.6 * jnp.exp(0.3 * t)) for a, t in zip(share, temp)),
        drift_ref[0],
        drift_ref[1],
    )
    for w, answer in enumerate(answers):
        answer_ref[pl.ds(w, blocks, stride=ANSWERED)] = answer
    spread = dot(
        jnp.concatenate(halves(answer_ref[...]), axis=1), jnp.concatenate([place, place], axis=0), NN
    )
    two = 2 * ANSWERED
    first = lax.broadcasted_iota(jnp.int32, (two, far * per_far), 0) // ANSWERED
    reply = jnp.zeros((two, far * per_far), jnp.float32)
    for b in range(0, blocks, 2):
        reply = reply + jnp.where(first == block - b, spread[b * ANSWERED:b * ANSWERED + two], 0.0)
    reply = reply + jnp.concatenate([reply[ANSWERED:], reply[:ANSWERED]], axis=0)
    turn = FAR_FIRST[1] - FAR_FIRST[0]
    order = [(g + turn) % far for g in range(far)]
    reply = jnp.concatenate([reply[:, g * per_far:(g + 1) * per_far] for g in order], axis=0)
    reply_ref[...] = reply.T.reshape(reply_ref.shape)


def finish_kernel(back_ref, slot_ref, off_ref, fac_ref, kelvin_ref, out_hbm, kelvin_hbm, out_ref, flat_ref, sems):
    levels, rows, _ = off_ref.shape
    n = slot_ref.shape[1]
    blocks = n // LANES
    fields = rows // blocks
    far = back_ref.shape[0] // ANSWERED
    for t in range(blocks):
        flat_ref[:, t * LANES:(t + 1) * LANES] = kelvin_ref[:, t]
    save_kelvin = pltpu.make_async_copy(flat_ref, kelvin_hbm, sems.at[0])
    save_kelvin.start()
    row = (slot_ref[0:1] + (far + FAR_FIRST[0] - FAR_FIRST[1])) % far
    place = one_hot(slot_ref[1:2], LANES)
    spread = dot(jnp.concatenate(halves(back_ref[...]), axis=1), jnp.concatenate([place, place], axis=0), NN)
    two = 2 * ANSWERED
    first = lax.broadcasted_iota(jnp.int32, (two, n), 0) // ANSWERED
    level = jnp.zeros((two, n), jnp.float32)
    for g in range(0, far, 2):
        level = level + jnp.where(first == row - g, spread[g * ANSWERED:g * ANSWERED + two], 0.0)
    level = level[:ANSWERED] + level[ANSWERED:]
    level = jnp.concatenate([level[0:fields, t * LANES:(t + 1) * LANES] for t in range(blocks)], axis=0)
    saves = []
    step = levels // PIECES
    for k in range(levels - 1, -1, -1):
        level = off_ref[k] + fac_ref[k] * level
        out_ref[k] = level
        if k % step == 0:
            part = pl.ds(k, step)
            save = pltpu.make_async_copy(out_ref.at[part], out_hbm.at[part], sems.at[1 + k // step])
            save.start()
            saves.append(save)
    for save in saves:
        save.wait()
    save_kelvin.wait()


def call(kernel, out_shape, in_space, out_spaces, scratch, *args):
    if in_space == pltpu.HBM:
        args = [pltpu.with_memory_space_constraint(x, pltpu.HBM) for x in args]
    return pl.pallas_call(
        kernel,
        out_shape=out_shape,
        in_specs=[pl.BlockSpec(memory_space=in_space)] * len(args),
        out_specs=[pl.BlockSpec(memory_space=space) for space in out_spaces],
        scratch_shapes=scratch,
        compiler_params=pltpu.CompilerParams(vmem_limit_bytes=32 * 1024 * 1024),
    )(*args)


def groups_of(far, near, far_first):
    far_order = [(k + far_first) % far for k in range(far)]
    near_order = [(k + NEAR_FIRST) % near for k in range(near)]
    return (
        [[f * near + q for f in far_order] for q in range(near)],
        [[f * near + q for q in near_order] for f in range(far)],
    )


def swap(parcels, groups):
    return lax.all_to_all(parcels, ("gx", "gy", "sa"), 0, 0, axis_index_groups=groups, tiled=True)


def send_to_cells(parcels, near):
    far, words, _ = parcels.shape
    far_groups, near_groups = groups_of(far, near, FAR_FIRST[0])
    parcels = jnp.pad(swap(parcels, far_groups), ((0, 0), (0, WORDS - words), (0, 0)))
    parcels = parcels.reshape(far * WORDS, near * CAP).T.reshape(near, CAP, far * WORDS)
    return swap(parcels, near_groups)


def send_back(parcels):
    near, cap, width = parcels.shape
    far = width // WORDS
    far_groups, near_groups = groups_of(far, near, FAR_FIRST[1])
    parcels = swap(parcels, near_groups).reshape(near * cap, width).T.reshape(far, WORDS, near * cap)
    return swap(parcels[:, :ANSWERED], far_groups).reshape(far * ANSWERED, near * cap)


def blocked(x):
    levels, fields, n = x.shape
    x = x.reshape(levels, fields, n // LANES, LANES).transpose(0, 2, 1, 3)
    return x.reshape(levels, fields * n // LANES, LANES)


def unblocked(x, fields):
    levels, rows, _ = x.shape
    x = x.reshape(levels, rows // fields, fields, LANES).transpose(0, 2, 1, 3)
    return x.reshape(levels, fields, rows * LANES // fields)


def per_device(profile, coefficients, owner, fractions, flags, flux, links, bottom, drift):
    far = lax.axis_size("gx")
    near = lax.axis_size(("gy", "sa"))
    fields, n = profile.shape[1:]
    profile, coefficients = blocked(profile), blocked(coefficients)
    f32, i32 = jnp.float32, jnp.int32
    shape = jax.ShapeDtypeStruct
    like = lambda x: shape(x.shape, x.dtype)
    held = lambda x: pltpu.VMEM(x.shape, x.dtype)
    vmem, hbm = pltpu.VMEM, pltpu.HBM
    offsets, factors, send, slot, *cells = call(
        lambda *refs: columns_kernel(far, near, *refs),
        [
            like(profile),
            like(profile),
            shape((far, SENT, near * CAP), f32),
            shape((2, n), i32),
            *[shape((x.shape[0], n // LANES, LANES), f32) for x in (fractions, flux, links, bottom, drift)],
        ],
        hbm,
        [vmem] * 9,
        [held(x) for x in (profile, coefficients, owner, fractions, flags, flux, links, bottom, drift)]
        + [pltpu.SemaphoreType.DMA((7 + 2 * INP,))],
        profile, coefficients, owner, fractions, flags, flux, links, bottom, drift,
    )
    got = send_to_cells(send, near)
    kelvin, reply = call(
        cells_kernel,
        [like(cells[0]), like(got)],
        vmem,
        [vmem] * 2,
        [pltpu.VMEM((ANSWERED * n // LANES, LANES), f32)],
        got, *cells,
    )
    back = send_back(reply)
    advanced, kelvin = call(
        finish_kernel,
        [like(profile), like(bottom)],
        vmem,
        [hbm] * 2,
        [held(profile), held(bottom), pltpu.SemaphoreType.DMA((1 + PIECES,))],
        back, slot, offsets, factors, kelvin,
    )
    return unblocked(advanced, fields), kelvin


def solution(mesh):
    spread3 = P(None, None, ("gx", "gy", "sa"))
    spread2 = P(None, ("gx", "gy", "sa"))
    return jax.shard_map(
        per_device,
        mesh=mesh,
        in_specs=(spread3, spread3) + (spread2,) * 7,
        out_specs=(spread3, spread2),
        check_vma=False,
    )
```

```python
import jax
import jax.numpy as jnp
from jax import lax
from jax.experimental import pallas as pl
from jax.experimental.pallas import tpu as pltpu
from jax.sharding import PartitionSpec as P

SWEEPS = 3
FAR_FIRST = (10, 10)
NEAR_FIRST = 22
WORDS = 8
SENT = 5
ANSWERED = 4
CAP = 4
LANES = 128
PIECES = 4
INP = 1
VAPOUR_ENTHALPY = 2.5
NT = (((1,), (1,)), ((), ()))
NN = (((1,), (0,)), ((), ()))


def halves(x):
    high = x.astype(jnp.bfloat16)
    return high, (x - high.astype(jnp.float32)).astype(jnp.bfloat16)


def stacked_halves(x):
    high = x.astype(jnp.bfloat16).astype(jnp.float32)
    return jnp.concatenate([high, x - high], axis=0)


def one_hot(index_row, count):
    ids = lax.broadcasted_iota(jnp.int32, (count, index_row.shape[1]), 0)
    return jnp.where(ids == index_row, 1.0, 0.0).astype(jnp.bfloat16)


def dot(a, b, dims):
    return lax.dot_general(a, b, dims, preferred_element_type=jnp.float32)


def columns_kernel(
    far,
    near,
    prof_hbm,
    coef_hbm,
    owner_hbm,
    fraction_hbm,
    flag_hbm,
    flux_hbm,
    link_hbm,
    bottom_hbm,
    drift_hbm,
    off_ref,
    fac_ref,
    send_ref,
    slot_ref,
    share_ref,
    base_ref,
    link_ref,
    bottom_ref,
    drift_ref,
    prof_ref,
    coef_ref,
    owner_ref,
    fraction_ref,
    flag_ref,
    flux_in,
    link_in,
    bottom_in,
    drift_in,
    sems,
):
    levels, rows, _ = prof_ref.shape
    n = owner_ref.shape[1]
    blocks = n // LANES
    fields = rows // blocks
    step = levels // INP
    parts = [pl.ds(k * step, step) for k in range(INP)]
    pairs = [(owner_hbm, owner_ref)]
    for part in parts:
        pairs += [(coef_hbm.at[part], coef_ref.at[part]), (prof_hbm.at[part], prof_ref.at[part])]
    pairs += [
        (fraction_hbm, fraction_ref),
        (flag_hbm, flag_ref),
        (flux_hbm, flux_in),
        (link_hbm, link_in),
        (bottom_hbm, bottom_in),
        (drift_hbm, drift_in),
    ]
    copies = [pltpu.make_async_copy(a, b, sems.at[k]) for k, (a, b) in enumerate(pairs)]
    for copy in copies:
        copy.start()
    copies[0].wait()
    owner = owner_ref[0:1, :]
    tall = jnp.concatenate([owner[:, j * LANES:(j + 1) * LANES] for j in range(blocks)], axis=0).T
    earlier = lax.broadcasted_iota(jnp.int32, (LANES, LANES), 0) < lax.broadcasted_iota(jnp.int32, (LANES, LANES), 1)
    totals = [jnp.zeros((1, LANES), jnp.int32) for _ in range(blocks)]
    for i in range(blocks):
        source = jnp.broadcast_to(tall[:, i:i + 1], (LANES, LANES))
        for j in range(i, blocks):
            same = source == owner[:, j * LANES:(j + 1) * LANES]
            if i == j:
                same = same & earlier
            totals[j] += jnp.sum(same.astype(jnp.int32), axis=0, keepdims=True)
    per_far = near * CAP
    row = (owner // near + (far - FAR_FIRST[0])) % far
    lane = (owner % near + (near - NEAR_FIRST)) % near * CAP + jnp.concatenate(totals, axis=1)
    slot_ref[0:1] = row
    slot_ref[1:2] = lane
    place = one_hot(lane, per_far)

    pair = lax.broadcasted_iota(jnp.int32, (8, LANES), 0) // 2
    above = last = before = shift = None
    for k in range(levels):
        if k % step == 0:
            copies[1 + 2 * (k // step)].wait()
            copies[2 + 2 * (k // step)].wait()
        below = jnp.concatenate(
            [
                jnp.take_along_axis(
                    coef_ref[k, 8 * (j // 2):8 * (j // 2) + 8], pair + 4 * (j % 2), axis=0, mode="promise_in_bounds"
                )
                for j in range(rows // 8)
            ],
            axis=0,
        )
        if k == 0:
            now, shift, numerator = 1.0 + below, prof_ref[k], below
        else:
            now = (1.0 + above + below) * last
            if k > 1:
                now = now - above * above * before
            else:
                now = now - above * above
            shift = prof_ref[k] * last + above * shift
            numerator = below * last
        inverse = 1.0 / now
        offset = shift * inverse
        factor = numerator * inverse
        off_ref[k] = offset
        fac_ref[k] = factor
        above, before, last = below, last, now

    values = []
    for t in range(blocks):
        at = fields * t
        code = (owner_ref[1:2, t * LANES:(t + 1) * LANES] + 1).astype(jnp.float32)
        values.append(
            jnp.concatenate(
                [offset[at:at + 2], factor[at:at + 1], below[at:at + 1], code, jnp.zeros((WORDS - 5, LANES), jnp.float32)],
                axis=0,
            )
        )
    values = stacked_halves(jnp.concatenate(values, axis=1))
    spread = jnp.concatenate([jnp.where(row == g, values, 0.0).astype(jnp.bfloat16) for g in range(far)], axis=0)
    sent = dot(spread, place, NT)
    for g in range(far):
        at = 2 * g * WORDS
        both = sent[at:at + SENT] + sent[at + WORDS:at + WORDS + SENT]
        for w in range(SENT):
            send_ref[g, w] = both[w:w + 1]

    rest = copies[1 + 2 * INP:]
    rest[0].wait()
    rest[1].wait()
    present = flag_ref[...].astype(jnp.float32)
    for t in range(blocks):
        part = slice(t * LANES, (t + 1) * LANES)
        share_ref[0:1, t] = fraction_ref[0:1, part]
        share_ref[1:, t] = fraction_ref[1:, part] * present[:, part]
    inverse = 1.0 / jnp.sum(share_ref[...], axis=0)
    for kind in range(share_ref.shape[0]):
        share_ref[kind] = share_ref[kind] * inverse
    for copy in rest[2:]:
        copy.wait()
    for t in range(blocks):
        part = slice(t * LANES, (t + 1) * LANES)
        link, bottom = link_in[:, part], bottom_in[:, part]
        base_ref[:, t] = flux_in[:, part] + link * bottom
        link_ref[:, t] = link
        bottom_ref[:, t] = bottom
        drift_ref[:, t] = drift_in[:, part]


def cells_kernel(got_ref, share_ref, base_ref, link_ref, bottom_ref, drift_ref, kelvin_ref, reply_ref, answer_ref):
    near, cap, width = got_ref.shape
    per_far = near * cap
    far = width // WORDS
    kinds, blocks, _ = share_ref.shape
    got = got_ref[...].reshape(per_far, far * WORDS).T
    high = got.astype(jnp.bfloat16).astype(jnp.float32)
    low = got - high
    word = lambda x, w: jnp.concatenate([x[g * WORDS + w:g * WORDS + w + 1] for g in range(far)], axis=1)
    cell = word(got, 4).astype(jnp.int32) - 1
    block = jnp.where(cell < 0, -1, cell // LANES)
    place = one_hot(cell % LANES, LANES)
    own = lax.broadcasted_iota(jnp.int32, (blocks, far * per_far), 0) == block
    spread = [jnp.where(own, word(x, w), 0.0) for w in range(4) for x in (high, low)]
    held = dot(jnp.concatenate(spread, axis=0).astype(jnp.bfloat16), place, NT)
    heat_offset, moist_offset, factor, exchange = (
        held[2 * w * blocks:(2 * w + 1) * blocks] + held[(2 * w + 1) * blocks:(2 * w + 2) * blocks] for w in range(4)
    )

    share = [share_ref[k] for k in range(kinds)]
    bottom = [bottom_ref[k] for k in range(kinds)]
    moist_pull = VAPOUR_ENTHALPY * exchange
    column_part = exchange * heat_offset + moist_pull * moist_offset
    heat_mix, moist_mix = exchange * factor, moist_pull * factor
    base = [base_ref[k] + column_part for k in range(kinds)]
    pull = [link_ref[k] + exchange for k in range(kinds)]
    temp = bottom
    for _ in range(SWEEPS):
        sat = [0.6 * jnp.exp(0.3 * t) for t in temp]
        emitted = [0.5 * jnp.exp(0.2 * t) for t in temp]
        mixed = heat_mix * sum(a * t for a, t in zip(share, temp)) + moist_mix * sum(a * q for a, q in zip(share, sat))
        for k in range(kinds):
            residual = (base[k] + mixed) - emitted[k] - pull[k] * temp[k] - moist_pull * sat[k]
            slope = 0.2 * emitted[k] + (0.3 * moist_pull) * sat[k] + pull[k]
            temp = temp[:k] + [temp[k] + residual / slope] + temp[k + 1:]
    for k in range(kinds):
        kelvin_ref[k] = temp[k]
    answers = (
        sum(a * t for a, t in zip(share, temp)),
        sum(a * (0.6 * jnp.exp(0.3 * t)) for a, t in zip(share, temp)),
        drift_ref[0],
        drift_ref[1],
    )
    for w, answer in enumerate(answers):
        answer_ref[pl.ds(w, blocks, stride=ANSWERED)] = answer
    spread = dot(
        jnp.concatenate(halves(answer_ref[...]), axis=1), jnp.concatenate([place, place], axis=0), NN
    )
    two = 2 * ANSWERED
    first = lax.broadcasted_iota(jnp.int32, (two, far * per_far), 0) // ANSWERED
    reply = jnp.zeros((two, far * per_far), jnp.float32)
    for b in range(0, blocks, 2):
        reply = reply + jnp.where(first == block - b, spread[b * ANSWERED:b * ANSWERED + two], 0.0)
    reply = reply + jnp.concatenate([reply[ANSWERED:], reply[:ANSWERED]], axis=0)
    turn = FAR_FIRST[1] - FAR_FIRST[0]
    order = [(g + turn) % far for g in range(far)]
    reply = jnp.concatenate([reply[:, g * per_far:(g + 1) * per_far] for g in order], axis=0)
    reply_ref[...] = reply.T.reshape(reply_ref.shape)


def finish_kernel(back_ref, slot_ref, off_ref, fac_ref, kelvin_ref, out_hbm, kelvin_hbm, out_ref, flat_ref, sems):
    levels, rows, _ = off_ref.shape
    n = slot_ref.shape[1]
    blocks = n // LANES
    fields = rows // blocks
    far = back_ref.shape[0] // ANSWERED
    for t in range(blocks):
        flat_ref[:, t * LANES:(t + 1) * LANES] = kelvin_ref[:, t]
    save_kelvin = pltpu.make_async_copy(flat_ref, kelvin_hbm, sems.at[0])
    save_kelvin.start()
    row = (slot_ref[0:1] + (far + FAR_FIRST[0] - FAR_FIRST[1])) % far
    place = one_hot(slot_ref[1:2], LANES)
    spread = dot(jnp.concatenate(halves(back_ref[...]), axis=1), jnp.concatenate([place, place], axis=0), NN)
    two = 2 * ANSWERED
    first = lax.broadcasted_iota(jnp.int32, (two, n), 0) // ANSWERED
    level = jnp.zeros((two, n), jnp.float32)
    for g in range(0, far, 2):
        level = level + jnp.where(first == row - g, spread[g * ANSWERED:g * ANSWERED + two], 0.0)
    level = level[:ANSWERED] + level[ANSWERED:]
    level = jnp.concatenate([level[0:fields, t * LANES:(t + 1) * LANES] for t in range(blocks)], axis=0)
    saves = []
    step = levels // PIECES
    for k in range(levels - 1, -1, -1):
        level = off_ref[k] + fac_ref[k] * level
        out_ref[k] = level
        if k % step == 0:
            part = pl.ds(k, step)
            save = pltpu.make_async_copy(out_ref.at[part], out_hbm.at[part], sems.at[1 + k // step])
            save.start()
            saves.append(save)
    for save in saves:
        save.wait()
    save_kelvin.wait()


def call(kernel, out_shape, in_space, out_spaces, scratch, *args):
    if in_space == pltpu.HBM:
        args = [pltpu.with_memory_space_constraint(x, pltpu.HBM) for x in args]
    return pl.pallas_call(
        kernel,
        out_shape=out_shape,
        in_specs=[pl.BlockSpec(memory_space=in_space)] * len(args),
        out_specs=[pl.BlockSpec(memory_space=space) for space in out_spaces],
        scratch_shapes=scratch,
        compiler_params=pltpu.CompilerParams(vmem_limit_bytes=32 * 1024 * 1024),
    )(*args)


def groups_of(far, near, far_first):
    far_order = [(k + far_first) % far for k in range(far)]
    near_order = [(k + NEAR_FIRST) % near for k in range(near)]
    return (
        [[f * near + q for f in far_order] for q in range(near)],
        [[f * near + q for q in near_order] for f in range(far)],
    )


def swap(parcels, groups):
    return lax.all_to_all(parcels, ("gx", "gy", "sa"), 0, 0, axis_index_groups=groups, tiled=True)


def send_to_cells(parcels, near):
    far, words = parcels.shape[:2]
    far_groups, near_groups = groups_of(far, near, FAR_FIRST[0])
    parcels = jnp.pad(swap(parcels, far_groups).reshape(far, words, near * CAP), ((0, 0), (0, WORDS - words), (0, 0)))
    parcels = parcels.reshape(far * WORDS, near * CAP).T.reshape(near, CAP, far * WORDS)
    return swap(parcels, near_groups)


def send_back(parcels):
    near, cap, width = parcels.shape
    far = width // WORDS
    far_groups, near_groups = groups_of(far, near, FAR_FIRST[1])
    parcels = swap(parcels, near_groups).reshape(near * cap, width).T.reshape(far, WORDS, near * cap)
    return swap(parcels[:, :ANSWERED], far_groups).reshape(far * ANSWERED, near * cap)


def blocked(x):
    levels, fields, n = x.shape
    x = x.reshape(levels, fields, n // LANES, LANES).transpose(0, 2, 1, 3)
    return x.reshape(levels, fields * n // LANES, LANES)


def unblocked(x, fields):
    levels, rows, _ = x.shape
    x = x.reshape(levels, rows // fields, fields, LANES).transpose(0, 2, 1, 3)
    return x.reshape(levels, fields, rows * LANES // fields)


def per_device(profile, coefficients, owner, fractions, flags, flux, links, bottom, drift):
    far = lax.axis_size("gx")
    near = lax.axis_size(("gy", "sa"))
    fields, n = profile.shape[1:]
    profile, coefficients = blocked(profile), blocked(coefficients)
    f32, i32 = jnp.float32, jnp.int32
    shape = jax.ShapeDtypeStruct
    like = lambda x: shape(x.shape, x.dtype)
    held = lambda x: pltpu.VMEM(x.shape, x.dtype)
    vmem, hbm = pltpu.VMEM, pltpu.HBM
    offsets, factors, send, slot, *cells = call(
        lambda *refs: columns_kernel(far, near, *refs),
        [
            like(profile),
            like(profile),
            shape((far, SENT, 1, near * CAP), f32),
            shape((2, n), i32),
            *[shape((x.shape[0], n // LANES, LANES), f32) for x in (fractions, flux, links, bottom, drift)],
        ],
        hbm,
        [vmem] * 9,
        [held(x) for x in (profile, coefficients, owner, fractions, flags, flux, links, bottom, drift)]
        + [pltpu.SemaphoreType.DMA((7 + 2 * INP,))],
        profile, coefficients, owner, fractions, flags, flux, links, bottom, drift,
    )
    got = send_to_cells(send, near)
    kelvin, reply = call(
        cells_kernel,
        [like(cells[0]), like(got)],
        vmem,
        [vmem] * 2,
        [pltpu.VMEM((ANSWERED * n // LANES, LANES), f32)],
        got, *cells,
    )
    back = send_back(reply)
    advanced, kelvin = call(
        finish_kernel,
        [like(profile), like(bottom)],
        vmem,
        [hbm] * 2,
        [held(profile), held(bottom), pltpu.SemaphoreType.DMA((1 + PIECES,))],
        back, slot, offsets, factors, kelvin,
    )
    return unblocked(advanced, fields), kelvin


def solution(mesh):
    spread3 = P(None, None, ("gx", "gy", "sa"))
    spread2 = P(None, ("gx", "gy", "sa"))
    return jax.shard_map(
        per_device,
        mesh=mesh,
        in_specs=(spread3, spread3) + (spread2,) * 7,
        out_specs=(spread3, spread2),
        check_vma=False,
    )
```

```python
import jax
import jax.numpy as jnp
from jax import lax
from jax.experimental import pallas as pl
from jax.experimental.pallas import tpu as pltpu
from jax.sharding import PartitionSpec as P

SWEEPS = 3
FAR_FIRST = (10, 9)
NEAR_FIRST = 22
WORDS = 8
SENT = 5
ANSWERED = 4
CAP = 4
LANES = 128
PIECES = 4
INP = 1
VAPOUR_ENTHALPY = 2.5
NT = (((1,), (1,)), ((), ()))
NN = (((1,), (0,)), ((), ()))


def halves(x):
    high = x.astype(jnp.bfloat16)
    return high, (x - high.astype(jnp.float32)).astype(jnp.bfloat16)


def stacked_halves(x):
    high = x.astype(jnp.bfloat16).astype(jnp.float32)
    return jnp.concatenate([high, x - high], axis=0)


def one_hot(index_row, count):
    ids = lax.broadcasted_iota(jnp.int32, (count, index_row.shape[1]), 0)
    return jnp.where(ids == index_row, 1.0, 0.0).astype(jnp.bfloat16)


def dot(a, b, dims):
    return lax.dot_general(a, b, dims, preferred_element_type=jnp.float32)


def columns_kernel(
    far,
    near,
    prof_hbm,
    coef_hbm,
    owner_hbm,
    fraction_hbm,
    flag_hbm,
    flux_hbm,
    link_hbm,
    bottom_hbm,
    drift_hbm,
    off_ref,
    fac_ref,
    send_ref,
    slot_ref,
    share_ref,
    base_ref,
    link_ref,
    bottom_ref,
    drift_ref,
    prof_ref,
    coef_ref,
    owner_ref,
    fraction_ref,
    flag_ref,
    flux_in,
    link_in,
    bottom_in,
    drift_in,
    sems,
):
    levels, rows, _ = prof_ref.shape
    n = owner_ref.shape[1]
    blocks = n // LANES
    fields = rows // blocks
    step = levels // INP
    parts = [pl.ds(k * step, step) for k in range(INP)]
    pairs = [(owner_hbm, owner_ref)]
    for part in parts:
        pairs += [(coef_hbm.at[part], coef_ref.at[part]), (prof_hbm.at[part], prof_ref.at[part])]
    pairs += [
        (fraction_hbm, fraction_ref),
        (flag_hbm, flag_ref),
        (flux_hbm, flux_in),
        (link_hbm, link_in),
        (bottom_hbm, bottom_in),
        (drift_hbm, drift_in),
    ]
    copies = [pltpu.make_async_copy(a, b, sems.at[k]) for k, (a, b) in enumerate(pairs)]
    for copy in copies:
        copy.start()
    copies[0].wait()
    owner = owner_ref[0:1, :]
    tall = jnp.concatenate([owner[:, j * LANES:(j + 1) * LANES] for j in range(blocks)], axis=0).T
    earlier = lax.broadcasted_iota(jnp.int32, (LANES, LANES), 0) < lax.broadcasted_iota(jnp.int32, (LANES, LANES), 1)
    totals = [jnp.zeros((1, LANES), jnp.int32) for _ in range(blocks)]
    for i in range(blocks):
        source = jnp.broadcast_to(tall[:, i:i + 1], (LANES, LANES))
        for j in range(i, blocks):
            same = source == owner[:, j * LANES:(j + 1) * LANES]
            if i == j:
                same = same & earlier
            totals[j] += jnp.sum(same.astype(jnp.int32), axis=0, keepdims=True)
    per_far = near * CAP
    row = (owner // near + (far - FAR_FIRST[0])) % far
    lane = (owner % near + (near - NEAR_FIRST)) % near * CAP + jnp.concatenate(totals, axis=1)
    slot_ref[0:1] = row
    slot_ref[1:2] = lane
    place = one_hot(lane, per_far)

    pair = lax.broadcasted_iota(jnp.int32, (8, LANES), 0) // 2
    above = last = before = shift = None
    for k in range(levels):
        if k % step == 0:
            copies[1 + 2 * (k // step)].wait()
            copies[2 + 2 * (k // step)].wait()
        below = jnp.concatenate(
            [
                jnp.take_along_axis(
                    coef_ref[k, 8 * (j // 2):8 * (j // 2) + 8], pair + 4 * (j % 2), axis=0, mode="promise_in_bounds"
                )
                for j in range(rows // 8)
            ],
            axis=0,
        )
        if k == 0:
            now, shift, numerator = 1.0 + below, prof_ref[k], below
        else:
            now = (1.0 + above + below) * last
            if k > 1:
                now = now - above * above * before
            else:
                now = now - above * above
            shift = prof_ref[k] * last + above * shift
            numerator = below * last
        inverse = 1.0 / now
        offset = shift * inverse
        factor = numerator * inverse
        off_ref[k] = offset
        fac_ref[k] = factor
        above, before, last = below, last, now

    values = []
    for t in range(blocks):
        at = fields * t
        code = (owner_ref[1:2, t * LANES:(t + 1) * LANES] + 1).astype(jnp.float32)
        values.append(
            jnp.concatenate(
                [offset[at:at + 2], factor[at:at + 1], below[at:at + 1], code, jnp.zeros((WORDS - 5, LANES), jnp.float32)],
                axis=0,
            )
        )
    values = stacked_halves(jnp.concatenate(values, axis=1))
    spread = jnp.concatenate([jnp.where(row == g, values, 0.0).astype(jnp.bfloat16) for g in range(far)], axis=0)
    sent = dot(spread, place, NT)
    for g in range(far):
        at = 2 * g * WORDS
        both = sent[at:at + SENT] + sent[at + WORDS:at + WORDS + SENT]
        for w in range(SENT):
            send_ref[g, w] = both[w:w + 1]

    rest = copies[1 + 2 * INP:]
    rest[0].wait()
    rest[1].wait()
    present = flag_ref[...].astype(jnp.float32)
    for t in range(blocks):
        part = slice(t * LANES, (t + 1) * LANES)
        share_ref[0:1, t] = fraction_ref[0:1, part]
        share_ref[1:, t] = fraction_ref[1:, part] * present[:, part]
    inverse = 1.0 / jnp.sum(share_ref[...], axis=0)
    for kind in range(share_ref.shape[0]):
        share_ref[kind] = share_ref[kind] * inverse
    for copy in rest[2:]:
        copy.wait()
    for t in range(blocks):
        part = slice(t * LANES, (t + 1) * LANES)
        link, bottom = link_in[:, part], bottom_in[:, part]
        base_ref[:, t] = flux_in[:, part] + link * bottom
        link_ref[:, t] = link
        bottom_ref[:, t] = bottom
        drift_ref[:, t] = drift_in[:, part]


def cells_kernel(got_ref, share_ref, base_ref, link_ref, bottom_ref, drift_ref, kelvin_ref, reply_ref, answer_ref):
    near, cap, width = got_ref.shape
    per_far = near * cap
    far = width // WORDS
    kinds, blocks, _ = share_ref.shape
    got = got_ref[...].reshape(per_far, far * WORDS).T
    high = got.astype(jnp.bfloat16).astype(jnp.float32)
    low = got - high
    word = lambda x, w: jnp.concatenate([x[g * WORDS + w:g * WORDS + w + 1] for g in range(far)], axis=1)
    cell = word(got, 4).astype(jnp.int32) - 1
    block = jnp.where(cell < 0, -1, cell // LANES)
    place = one_hot(cell % LANES, LANES)
    own = lax.broadcasted_iota(jnp.int32, (blocks, far * per_far), 0) == block
    spread = [jnp.where(own, word(x, w), 0.0) for w in range(4) for x in (high, low)]
    held = dot(jnp.concatenate(spread, axis=0).astype(jnp.bfloat16), place, NT)
    heat_offset, moist_offset, factor, exchange = (
        held[2 * w * blocks:(2 * w + 1) * blocks] + held[(2 * w + 1) * blocks:(2 * w + 2) * blocks] for w in range(4)
    )

    share = [share_ref[k] for k in range(kinds)]
    bottom = [bottom_ref[k] for k in range(kinds)]
    moist_pull = VAPOUR_ENTHALPY * exchange
    column_part = exchange * heat_offset + moist_pull * moist_offset
    heat_mix, moist_mix = exchange * factor, moist_pull * factor
    base = [base_ref[k] + column_part for k in range(kinds)]
    pull = [link_ref[k] + exchange for k in range(kinds)]
    temp = bottom
    for _ in range(SWEEPS):
        sat = [0.6 * jnp.exp(0.3 * t) for t in temp]
        emitted = [0.5 * jnp.exp(0.2 * t) for t in temp]
        mixed = heat_mix * sum(a * t for a, t in zip(share, temp)) + moist_mix * sum(a * q for a, q in zip(share, sat))
        for k in range(kinds):
            residual = (base[k] + mixed) - emitted[k] - pull[k] * temp[k] - moist_pull * sat[k]
            slope = 0.2 * emitted[k] + (0.3 * moist_pull) * sat[k] + pull[k]
            temp = temp[:k] + [temp[k] + residual / slope] + temp[k + 1:]
    for k in range(kinds):
        kelvin_ref[k] = temp[k]
    answers = (
        sum(a * t for a, t in zip(share, temp)),
        sum(a * (0.6 * jnp.exp(0.3 * t)) for a, t in zip(share, temp)),
        drift_ref[0],
        drift_ref[1],
    )
    for w, answer in enumerate(answers):
        answer_ref[pl.ds(w, blocks, stride=ANSWERED)] = answer
    spread = dot(
        jnp.concatenate(halves(answer_ref[...]), axis=1), jnp.concatenate([place, place], axis=0), NN
    )
    two = 2 * ANSWERED
    first = lax.broadcasted_iota(jnp.int32, (two, far * per_far), 0) // ANSWERED
    reply = jnp.zeros((two, far * per_far), jnp.float32)
    for b in range(0, blocks, 2):
        reply = reply + jnp.where(first == block - b, spread[b * ANSWERED:b * ANSWERED + two], 0.0)
    reply = reply + jnp.concatenate([reply[ANSWERED:], reply[:ANSWERED]], axis=0)
    turn = FAR_FIRST[1] - FAR_FIRST[0]
    order = [(g + turn) % far for g in range(far)]
    reply = jnp.concatenate([reply[:, g * per_far:(g + 1) * per_far] for g in order], axis=0)
    reply_ref[...] = reply.T.reshape(reply_ref.shape)


def finish_kernel(back_ref, slot_ref, off_ref, fac_ref, kelvin_ref, out_hbm, kelvin_hbm, out_ref, flat_ref, sems):
    levels, rows, _ = off_ref.shape
    n = slot_ref.shape[1]
    blocks = n // LANES
    fields = rows // blocks
    far = back_ref.shape[0] // ANSWERED
    for t in range(blocks):
        flat_ref[:, t * LANES:(t + 1) * LANES] = kelvin_ref[:, t]
    save_kelvin = pltpu.make_async_copy(flat_ref, kelvin_hbm, sems.at[0])
    save_kelvin.start()
    row = (slot_ref[0:1] + (far + FAR_FIRST[0] - FAR_FIRST[1])) % far
    place = one_hot(slot_ref[1:2], LANES)
    spread = dot(jnp.concatenate(halves(back_ref[...]), axis=1), jnp.concatenate([place, place], axis=0), NN)
    two = 2 * ANSWERED
    first = lax.broadcasted_iota(jnp.int32, (two, n), 0) // ANSWERED
    level = jnp.zeros((two, n), jnp.float32)
    for g in range(0, far, 2):
        level = level + jnp.where(first == row - g, spread[g * ANSWERED:g * ANSWERED + two], 0.0)
    level = level[:ANSWERED] + level[ANSWERED:]
    level = jnp.concatenate([level[0:fields, t * LANES:(t + 1) * LANES] for t in range(blocks)], axis=0)
    saves = []
    step = levels // PIECES
    for k in range(levels - 1, -1, -1):
        level = off_ref[k] + fac_ref[k] * level
        out_ref[k] = level
        if k % step == 0:
            part = pl.ds(k, step)
            save = pltpu.make_async_copy(out_ref.at[part], out_hbm.at[part], sems.at[1 + k // step])
            save.start()
            saves.append(save)
    for save in saves:
        save.wait()
    save_kelvin.wait()


def call(kernel, out_shape, in_space, out_spaces, scratch, *args):
    if in_space == pltpu.HBM:
        args = [pltpu.with_memory_space_constraint(x, pltpu.HBM) for x in args]
    return pl.pallas_call(
        kernel,
        out_shape=out_shape,
        in_specs=[pl.BlockSpec(memory_space=in_space)] * len(args),
        out_specs=[pl.BlockSpec(memory_space=space) for space in out_spaces],
        scratch_shapes=scratch,
        compiler_params=pltpu.CompilerParams(vmem_limit_bytes=32 * 1024 * 1024),
    )(*args)


def groups_of(far, near, far_first):
    far_order = [(k + far_first) % far for k in range(far)]
    near_order = [(k + NEAR_FIRST) % near for k in range(near)]
    return (
        [[f * near + q for f in far_order] for q in range(near)],
        [[f * near + q for q in near_order] for f in range(far)],
    )


def swap(parcels, groups):
    return lax.all_to_all(parcels, ("gx", "gy", "sa"), 0, 0, axis_index_groups=groups, tiled=True)


def send_to_cells(parcels, near):
    far, words = parcels.shape[:2]
    far_groups, near_groups = groups_of(far, near, FAR_FIRST[0])
    parcels = jnp.pad(swap(parcels, far_groups).reshape(far, words, near * CAP), ((0, 0), (0, WORDS - words), (0, 0)))
    parcels = parcels.reshape(far * WORDS, near * CAP).T.reshape(near, CAP, far * WORDS)
    return swap(parcels, near_groups)


def send_back(parcels):
    near, cap, width = parcels.shape
    far = width // WORDS
    far_groups, near_groups = groups_of(far, near, FAR_FIRST[1])
    parcels = swap(parcels, near_groups).reshape(near * cap, width).T.reshape(far, WORDS, near * cap)
    return swap(parcels[:, :ANSWERED], far_groups).reshape(far * ANSWERED, near * cap)


def blocked(x):
    levels, fields, n = x.shape
    x = x.reshape(levels, fields, n // LANES, LANES).transpose(0, 2, 1, 3)
    return x.reshape(levels, fields * n // LANES, LANES)


def unblocked(x, fields):
    levels, rows, _ = x.shape
    x = x.reshape(levels, rows // fields, fields, LANES).transpose(0, 2, 1, 3)
    return x.reshape(levels, fields, rows * LANES // fields)


def per_device(profile, coefficients, owner, fractions, flags, flux, links, bottom, drift):
    far = lax.axis_size("gx")
    near = lax.axis_size(("gy", "sa"))
    fields, n = profile.shape[1:]
    profile, coefficients = blocked(profile), blocked(coefficients)
    f32, i32 = jnp.float32, jnp.int32
    shape = jax.ShapeDtypeStruct
    like = lambda x: shape(x.shape, x.dtype)
    held = lambda x: pltpu.VMEM(x.shape, x.dtype)
    vmem, hbm = pltpu.VMEM, pltpu.HBM
    offsets, factors, send, slot, *cells = call(
        lambda *refs: columns_kernel(far, near, *refs),
        [
            like(profile),
            like(profile),
            shape((far, SENT, 1, near * CAP), f32),
            shape((2, n), i32),
            *[shape((x.shape[0], n // LANES, LANES), f32) for x in (fractions, flux, links, bottom, drift)],
        ],
        hbm,
        [vmem] * 9,
        [held(x) for x in (profile, coefficients, owner, fractions, flags, flux, links, bottom, drift)]
        + [pltpu.SemaphoreType.DMA((7 + 2 * INP,))],
        profile, coefficients, owner, fractions, flags, flux, links, bottom, drift,
    )
    got = send_to_cells(send, near)
    kelvin, reply = call(
        cells_kernel,
        [like(cells[0]), like(got)],
        vmem,
        [vmem] * 2,
        [pltpu.VMEM((ANSWERED * n // LANES, LANES), f32)],
        got, *cells,
    )
    back = send_back(reply)
    advanced, kelvin = call(
        finish_kernel,
        [like(profile), like(bottom)],
        vmem,
        [hbm] * 2,
        [held(profile), held(bottom), pltpu.SemaphoreType.DMA((1 + PIECES,))],
        back, slot, offsets, factors, kelvin,
    )
    return unblocked(advanced, fields), kelvin


def solution(mesh):
    spread3 = P(None, None, ("gx", "gy", "sa"))
    spread2 = P(None, ("gx", "gy", "sa"))
    return jax.shard_map(
        per_device,
        mesh=mesh,
        in_specs=(spread3, spread3) + (spread2,) * 7,
        out_specs=(spread3, spread2),
        check_vma=False,
    )
```
